256 devices in a mesh: pole: 2 (over x_hi), fy: 8 (over z), fz: 16 (over y, x_lo, core).
Axes of the slice: x: 4 (x_hi: 2, x_lo: 2; x = x_hi * 2 + x_lo), y: 4, z: 8, core: 2. Of those that a mesh axis runs over, the one named last changes fastest.
Arguments:
- states: float32 [2, 128, 128, 256], P(None, 'fy', 'fz'), may hold values from -126 to 126
- potential: float32 [128, 128, 256], P('fy', 'fz'), may hold values from 0.5 to 3
Outputs:
- filtered: float32 [2, 128, 128, 256], P('pole', 'fy', 'fz')
- correlation_gram: float32 [2, 2], replicated
- energy_gram: float32 [2, 2], replicated
The draws below stay inside these ranges and needn't reach their ends.
All inputs are finite; a program needn't handle non-finite values.
Results may differ from the reference program's by a relative error of at most 0.0003.
Values sent between devices are 32-bit elements; how exact they have to be, the bound alone decides.
A program may use at most 64 MiB of HBM per device.

```python
import math
import jax
import jax.numpy as jnp
from jax import lax

NX = 256
NY = 128
NZ = 128
COLS = 2
ITERS = 2
N_POLE = 2


def draw_states(key, part):
    key = jax.random.fold_in(key, 11)
    along_y = (jnp.arange(NY).astype(jnp.float32) / NY)[None, :, None, None]
    along_z = (jnp.arange(NZ).astype(jnp.float32) / NZ)[None, None, :, None]
    envelope = jnp.exp(math.log(3.0) * (along_y + along_z) * 0.5)
    noise = jnp.clip(jax.random.normal(key, (COLS, NY, NZ, NX), jnp.float32), -6.0, 6.0)
    return (4.0 * envelope * noise).astype(jnp.float32)


def levels(stream_key, dims, pieces, low, top_value):
    factor_of, own = 1.0, jax.random.fold_in(stream_key, 6)
    for position, parts in pieces:
        heights = jnp.exp(jax.random.uniform(jax.random.fold_in(own, position), (parts,), jnp.float32, low / len(pieces), top_value / len(pieces)))
        factor_of = factor_of * jnp.repeat(heights, dims[position] // parts).reshape([-1 if axis == position else 1 for axis in range(len(dims))])
    return factor_of


def setup_inputs(seed: int = 0) -> dict:
    key_list = jax.random.split(jax.random.key(seed), 3)
    return {
        "states": draw_states(jax.random.fold_in(key_list[2], 71), 0),
        "potential": jnp.clip(0.5 + 2.5 * jax.random.uniform(key_list[1], (NY, NZ, NX), jnp.float32) ** levels(key_list[1], (NY, NZ, NX), ((0, 8), (1, 16)), -0.2, 0.2), 0.5, 3.0),
    }


center_energy = 1.0
contour_radius = 1.0


def squares_of_frequency(length):
    indices = jnp.arange(length)
    signed = jnp.where(indices < length // 2, indices, indices - length).astype(jnp.float32) * (2.0 * math.pi / length)
    return signed * signed


def kinetic_table():
    return 0.5 * (squares_of_frequency(NY)[:, None, None] + squares_of_frequency(NZ)[None, :, None] + squares_of_frequency(NX)[None, None, :])


def hamiltonian(vectors, potential, kinetic):
    spectrum = jnp.fft.fftn(vectors, axes=(1, 2, 3))
    return jnp.fft.ifftn(spectrum * kinetic, axes=(1, 2, 3)) + potential * vectors


def bilinear(left, right):
    return jnp.sum(left * right, axis=(1, 2, 3))


def reference(states, potential):
    kinetic = kinetic_table()
    filtered = jnp.zeros(states.shape, jnp.float32)
    for pole_index in range(N_POLE):
        pole_angle = math.pi * (pole_index + 0.5) / N_POLE
        rotation = complex(math.cos(pole_angle), math.sin(pole_angle))
        shift_value = center_energy + contour_radius * rotation
        weight = contour_radius * rotation / N_POLE
        solution = 0.0 * shift_value * states
        residual = states
        direction = states
        res_norm = bilinear(residual, residual)
        for iteration in range(ITERS):
            shifted_image = shift_value * direction - hamiltonian(direction, potential, kinetic)
            step_size = res_norm / bilinear(direction, shifted_image)
            solution = solution + step_size[:, None, None, None] * direction
            residual = residual - step_size[:, None, None, None] * shifted_image
            if iteration + 1 < ITERS:
                next_norm = bilinear(residual, residual)
                direction = residual + (next_norm / res_norm)[:, None, None, None] * direction
                res_norm = next_norm
        filtered = filtered + jnp.real(weight * solution)
    applied = jnp.real(hamiltonian(filtered, potential, kinetic))
    cell_count = NX * NY * NZ
    correlation_gram = jnp.einsum("iyzx,jyzx->ij", filtered, filtered, precision=lax.Precision.HIGHEST) / cell_count
    energy_gram = jnp.einsum("iyzx,jyzx->ij", filtered, applied, precision=lax.Precision.HIGHEST) / cell_count
    return filtered, correlation_gram, energy_gram
```

```python
import functools
import math

import jax
import jax.numpy as jnp
import numpy as np
from jax import lax
from jax.experimental import pallas as pl
from jax.experimental.pallas import tpu as pltpu
from jax.sharding import PartitionSpec as P

MESH = pl.DeviceIdType.MESH
HIGH = lax.Precision.HIGHEST


def axis_operator(length):
    index = np.arange(length)
    signed = np.where(index < length // 2, index, index - length) * (2.0 * math.pi / length)
    phases = (index[:, None] * index[None, :] % length) * (2.0 * math.pi / length)
    first = (np.cos(phases) @ (0.5 * signed * signed)) / length
    return np.asarray(first[(index[:, None] - index[None, :]) % length], np.float32)


def dot(left, right):
    return jnp.dot(left, right, precision=HIGH, preferred_element_type=jnp.float32)


def lanes(product):
    total = jnp.sum(product, axis=0, keepdims=True)
    return sum(total[:, i : i + 128] for i in range(0, total.shape[1], 128))


def kernel(
    cy, cz, nx, fy, fz,
    states_ref, pot_ref, dx_ref, dy_ref, dz_ref,
    out_ref, corr_ref, energy_ref,
    b_ref, ysend, yb, zb, ymul, zmul, yback, zback, s_ref, u_ref, yusend, yu, zu,
    acc1, acc2, sum1, sum2, part1, part2, part1z, part2z,
    send_sem, recv_sem,
):
    pole, my, mz = lax.axis_index("pole"), lax.axis_index("fy"), lax.axis_index("fz")
    rows = cy * cz
    wide = 2 * nx
    first, second = slice(0, nx), slice(nx, wide)

    def at_y(index):
        return (pole, index, mz)

    def at_z(index):
        return (pole, my, index)

    def chunk(index, size):
        return pl.ds(pl.multiple_of(index * size, size), size)

    def scatter(src, dst, size, count, me, place, slot, broadcast=False):
        def body(step, carry):
            other = lax.rem(me + step, count)
            pltpu.make_async_remote_copy(
                src_ref=src if broadcast else src.at[chunk(other, size)],
                dst_ref=dst.at[chunk(me, size)],
                send_sem=send_sem.at[slot],
                recv_sem=recv_sem.at[slot],
                device_id=place(other),
                device_id_type=MESH,
            ).start()
            return carry

        lax.fori_loop(1, count, body, 0)
        dst[chunk(me, size)] = src[...] if broadcast else src[chunk(me, size)]

    def arrived(dst, size, count, slot):
        whole = dst.at[pl.ds(0, (count - 1) * size)]
        pltpu.make_async_copy(whole, whole, recv_sem.at[slot]).wait()

    def sent(dst, size, count, slot):
        whole = dst.at[pl.ds(0, (count - 1) * size)]
        pltpu.make_async_copy(whole, whole, send_sem.at[slot]).wait()

    barrier = pltpu.get_barrier_semaphore()

    def greet_y(step, carry):
        pl.semaphore_signal(
            barrier, inc=1, device_id=at_y(lax.rem(my + step, fy)), device_id_type=MESH
        )
        return carry

    def greet_z(step, carry):
        pl.semaphore_signal(
            barrier, inc=1, device_id=at_z(lax.rem(mz + step, fz)), device_id_type=MESH
        )
        return carry

    lax.fori_loop(1, fy, greet_y, 0)
    lax.fori_loop(1, fz, greet_z, 0)

    b_ref[:, first] = states_ref[0].reshape(rows, nx)
    b_ref[:, second] = states_ref[1].reshape(rows, nx)

    def swapped(value, major, minor):
        return jnp.swapaxes(value.reshape(major, minor, wide), 0, 1).reshape(rows, wide)

    ysend[...] = swapped(b_ref[...], cy, cz)
    pl.semaphore_wait(barrier, fy + fz - 2)

    scatter(ysend, yb, cy, fy, my, at_y, 0)
    scatter(b_ref, zb, cz, fz, mz, at_z, 1)

    b0, b1 = b_ref[:, first], b_ref[:, second]
    v = pot_ref[...].reshape(rows, nx)
    s_ref[:, first] = v * b0 + dot(b0, dx_ref[...])
    s_ref[:, second] = v * b1 + dot(b1, dx_ref[...])
    acc1[0:1] = lanes(b0 * b0)
    acc1[1:2] = lanes(b0 * b1)
    acc1[2:3] = lanes(b1 * b1)
    acc1[5:8] = jnp.zeros((3, 128), jnp.float32)
    own0 = lanes(b0 * s_ref[:, first])
    own1 = lanes(b1 * s_ref[:, second])

    arrived(zb, cz, fz, 1)
    zmul[...] = dot(dz_ref[...], zb[...])
    scatter(zmul, zback, cz, fz, mz, at_z, 3)
    arrived(yb, cy, fy, 0)
    ymul[...] = dot(dy_ref[...], yb[...])
    scatter(ymul, yback, cy, fy, my, at_y, 2)

    zz = zb[...] * zmul[...]
    yy = yb[...] * ymul[...]
    acc1[3:4] = own0 + lanes(zz[:, first]) + lanes(yy[:, first])
    acc1[4:5] = own1 + lanes(zz[:, second]) + lanes(yy[:, second])
    scatter(acc1, part1, 8, fy, my, at_y, 6, True)

    arrived(zback, cz, fz, 3)
    s_ref[...] += zback[...]
    arrived(part1, 8, fy, 6)
    sum1[...] = sum(part1[8 * i : 8 * i + 8] for i in range(fy))
    scatter(sum1, part1z, 8, fz, mz, at_z, 7, True)
    arrived(yback, cy, fy, 2)
    u_ref[...] = s_ref[...] + swapped(yback[...], cz, cy)
    scatter(u_ref, zu, cz, fz, mz, at_z, 5)
    yusend[...] = swapped(u_ref[...], cy, cz)
    scatter(yusend, yu, cy, fy, my, at_y, 4)

    arrived(part1z, 8, fz, 7)
    total1 = jnp.sum(sum(part1z[8 * i : 8 * i + 8] for i in range(fz)), axis=1, keepdims=True)
    m00, m01, m11 = total1[0:1], total1[1:2], total1[2:3]
    mu0, mu1 = total1[3:4] / m00, total1[4:5] / m11

    w0 = u_ref[:, first] - mu0 * b0
    w1 = u_ref[:, second] - mu1 * b1
    s_ref[:, first] = w0
    s_ref[:, second] = w1
    t0 = v * w0 + dot(w0, dx_ref[...])
    t1 = v * w1 + dot(w1, dx_ref[...])
    acc2[0:1] = lanes(w0 * w0)
    acc2[1:2] = lanes(w0 * w1)
    acc2[2:3] = lanes(w1 * w1)
    acc2[6:7] = lanes(b0 * w0)
    acc2[7:8] = lanes(b0 * w1)
    acc2[8:9] = lanes(b1 * w0)
    acc2[9:10] = lanes(b1 * w1)
    acc2[10:16] = jnp.zeros((6, 128), jnp.float32)
    h00, h01, h11 = lanes(w0 * t0), lanes(w0 * t1), lanes(w1 * t1)

    def quadratic(operator, pencil, base):
        left0 = pencil[:, first] - mu0 * base[:, first]
        left1 = pencil[:, second] - mu1 * base[:, second]
        right0 = dot(operator[...], left0)
        right1 = dot(operator[...], left1)
        return lanes(left0 * right0), lanes(left0 * right1), lanes(left1 * right1)

    arrived(zu, cz, fz, 5)
    z00, z01, z11 = quadratic(dz_ref, zu, zb)
    arrived(yu, cy, fy, 4)
    y00, y01, y11 = quadratic(dy_ref, yu, yb)
    acc2[3:4] = h00 + z00 + y00
    acc2[4:5] = h01 + z01 + y01
    acc2[5:6] = h11 + z11 + y11

    scatter(acc2, part2, 16, fy, my, at_y, 8, True)
    arrived(part2, 16, fy, 8)
    sum2[...] = sum(part2[16 * i : 16 * i + 16] for i in range(fy))
    scatter(sum2, part2z, 16, fz, mz, at_z, 9, True)
    arrived(part2z, 16, fz, 9)
    total2 = jnp.sum(sum(part2z[16 * i : 16 * i + 16] for i in range(fz)), axis=1, keepdims=True)
    w00, w01, w11, e00, e01, e11, c00, c01, c10, c11 = (total2[i : i + 1] for i in range(10))

    def factors(mu, norm, ww, whw):
        nu = jnp.where(ww > 0.0, whw / jnp.where(ww > 0.0, ww, 1.0), mu)
        t2 = ww / norm
        p, q = mu - 1.0, nu - 1.0
        trace, det = p + q, p * q - t2
        real, imag = det * det - 1.0, 2.0 * det - trace * trace
        size = real * real + imag * imag
        return ((det - q * trace) * imag - real) / size, trace * imag / size

    a0, f0 = factors(mu0, m00, w00, e00)
    a1, f1 = factors(mu1, m11, w11, e11)
    own = pole == 0
    out = jnp.where(own, a0, a1) * jnp.where(own, b0, b1) + jnp.where(own, f0, f1) * jnp.where(
        own, w0, w1
    )
    out_ref[0] = out.reshape(cy, cz, nx)

    cells = 1.0 / float(nx * cy * fy * cz * fz)

    def correlation(ai, fi, aj, fj, bb, biwj, bjwi, ww):
        return (ai * aj * bb + ai * fj * biwj + fi * aj * bjwi + fi * fj * ww) * cells

    def energy(ai, fi, aj, fj, mui, muj, bb, biwj, bjwi, ww, whw):
        bhb = biwj + muj * bb
        bihwj = ww + mui * biwj
        wihbj = ww + muj * bjwi
        return (ai * aj * bhb + ai * fj * bihwj + fi * aj * wihbj + fi * fj * whw) * cells

    cross = correlation(a0, f0, a1, f1, m01, c01, c10, w01)
    corr_ref[0:1, 0:1] = correlation(a0, f0, a0, f0, m00, c00, c00, w00)
    corr_ref[0:1, 1:2] = cross
    corr_ref[1:2, 0:1] = cross
    corr_ref[1:2, 1:2] = correlation(a1, f1, a1, f1, m11, c11, c11, w11)
    cross = energy(a0, f0, a1, f1, mu0, mu1, m01, c01, c10, w01, e01)
    energy_ref[0:1, 0:1] = energy(a0, f0, a0, f0, mu0, mu0, m00, c00, c00, w00, e00)
    energy_ref[0:1, 1:2] = cross
    energy_ref[1:2, 0:1] = cross
    energy_ref[1:2, 1:2] = energy(a1, f1, a1, f1, mu1, mu1, m11, c11, c11, w11, e11)

    sent(yb, cy, fy, 0)
    sent(zb, cz, fz, 1)
    sent(yback, cy, fy, 2)
    sent(zback, cz, fz, 3)
    sent(yu, cy, fy, 4)
    sent(zu, cz, fz, 5)
    sent(part1, 8, fy, 6)
    sent(part1z, 8, fz, 7)
    sent(part2, 16, fy, 8)
    sent(part2z, 16, fz, 9)


def local(states, potential):
    columns, cy, cz, nx = states.shape
    fy, fz = lax.axis_size("fy"), lax.axis_size("fz")
    rows = cy * cz
    block = pltpu.VMEM((rows, columns * nx), jnp.float32)
    f32 = jnp.float32
    in_vmem = pl.BlockSpec(memory_space=pltpu.VMEM)
    return pl.pallas_call(
        functools.partial(kernel, cy, cz, nx, fy, fz),
        out_shape=(
            jax.ShapeDtypeStruct((1, cy, cz, nx), f32),
            jax.ShapeDtypeStruct((columns, columns), f32),
            jax.ShapeDtypeStruct((columns, columns), f32),
        ),
        in_specs=[in_vmem] * 5,
        out_specs=(in_vmem,) * 3,
        scratch_shapes=[block] * 13
        + [
            pltpu.VMEM((8, 128), f32),
            pltpu.VMEM((16, 128), f32),
            pltpu.VMEM((8, 128), f32),
            pltpu.VMEM((16, 128), f32),
            pltpu.VMEM((8 * fy, 128), f32),
            pltpu.VMEM((16 * fy, 128), f32),
            pltpu.VMEM((8 * fz, 128), f32),
            pltpu.VMEM((16 * fz, 128), f32),
            pltpu.SemaphoreType.DMA((10,)),
            pltpu.SemaphoreType.DMA((10,)),
        ],
        compiler_params=pltpu.CompilerParams(
            collective_id=0, has_side_effects=True, vmem_limit_bytes=32 * 1024 * 1024
        ),
    )(
        states,
        potential,
        jnp.asarray(axis_operator(nx)),
        jnp.asarray(axis_operator(cy * fy)),
        jnp.asarray(axis_operator(cz * fz)),
    )


def solution(mesh):
    placed = (P(None, "fy", "fz", None), P("fy", "fz", None))
    return jax.shard_map(
        local,
        mesh=mesh,
        in_specs=placed,
        out_specs=(P("pole", "fy", "fz", None), P(), P()),
        check_vma=False,
    )
```

```python
import functools
import math

import jax
import jax.numpy as jnp
import numpy as np
from jax import lax
from jax.experimental import pallas as pl
from jax.experimental.pallas import tpu as pltpu
from jax.sharding import PartitionSpec as P

MESH = pl.DeviceIdType.MESH
HIGH = lax.Precision.HIGHEST


def axis_operator(length):
    index = np.arange(length)
    signed = np.where(index < length // 2, index, index - length) * (2.0 * math.pi / length)
    phases = (index[:, None] * index[None, :] % length) * (2.0 * math.pi / length)
    first = (np.cos(phases) @ (0.5 * signed * signed)) / length
    return np.asarray(first[(index[:, None] - index[None, :]) % length], np.float32)


def far_first(count):
    return sorted(range(1, count), key=lambda k: -min(k, count - k))


def dot(left, right):
    return jnp.dot(left, right, precision=HIGH, preferred_element_type=jnp.float32)


def lanes(product):
    return jnp.sum(product, axis=0, keepdims=True)


def kernel(
    cy, cz, nx, fy, fz, poles,
    states_hbm, pot_hbm, dx_hbm, dy_hbm, dz_hbm,
    w_ref, coef_ref, corr_ref, energy_ref,
    own_b, far_b, v_ref, dx_ref, dy_ref, dz_ref, s_ref, u_ref,
    ysend, yb, zb, ymul, zmul, yback, zback, yusend, yu, zu, far_u, far_w,
    acc1, acc2, sum1, sum2, part1, part2, part1z, part2z,
    load_sem, send_sem, recv_sem,
):
    pole, my, mz = lax.axis_index("pole"), lax.axis_index("fy"), lax.axis_index("fz")
    partner = 1 - pole
    plane = pole * fz + mz
    rows = cy * cz
    half = nx // 2
    split = cy // 2
    col0, col1 = slice(0, half), slice(half, nx)

    def lane_block(index):
        return pl.ds(pl.multiple_of(index * half, half), half)

    def at_y(step):
        return (pole, lax.rem(my + step, fy), mz)

    def at_z(step):
        return (pole, my, lax.rem(mz + step, fz))

    def at_plane(step):
        other = lax.rem(plane + step, poles * fz)
        return (other // fz, my, lax.rem(other, fz))

    def push(src, dst, place, slot):
        pltpu.make_async_remote_copy(
            src_ref=src,
            dst_ref=dst,
            send_sem=send_sem.at[slot],
            recv_sem=recv_sem.at[slot],
            device_id=place,
            device_id_type=MESH,
        ).start()

    def push_y(src, dst, step, slot):
        push(src.at[lax.rem(my + step, fy)], dst.at[my], at_y(step), slot)

    def push_z(src, dst, step, slot):
        push(src.at[lax.rem(mz + step, fz)], dst.at[mz], at_z(step), slot)

    def exchange(ysrc, ydst, yslot, zsrc, zdst, zslot):
        ysteps, zsteps = far_first(fy), far_first(fz)
        for i in range(max(fy, fz) - 1):
            if i < len(ysteps):
                push_y(ysrc, ydst, ysteps[i], yslot)
            if i < len(zsteps):
                push_z(zsrc, zdst, zsteps[i], zslot)
        ydst[my] = ysrc[my]
        zdst[mz] = zsrc[mz]

    def spread(src, dst, count, me, place, slot):
        def body(step, carry):
            push(src, dst.at[me], place(step), slot)
            return carry

        lax.fori_loop(1, count, body, 0)
        dst[me] = src[...]

    def arrived(dst, count, slot):
        whole = dst.at[pl.ds(0, count)]
        pltpu.make_async_copy(whole, whole, recv_sem.at[slot]).wait()

    def sent(dst, count, slot):
        whole = dst.at[pl.ds(0, count)]
        pltpu.make_async_copy(whole, whole, send_sem.at[slot]).wait()

    barrier = pltpu.get_barrier_semaphore()

    def greet(count, place):
        def body(step, carry):
            pl.semaphore_signal(barrier, inc=1, device_id=place(step), device_id_type=MESH)
            return carry

        lax.fori_loop(1, count, body, 0)

    greet(fy, at_y)
    greet(poles * fz, at_plane)

    def load(src, dst, slot):
        copy = pltpu.make_async_copy(src, dst, load_sem.at[slot])
        copy.start()
        return copy

    near = [load(states_hbm.at[c, :, :, lane_block(pole)], own_b.at[:, :, pl.ds(c * half, half)], c) for c in range(2)]
    rest = [
        load(states_hbm.at[c, :, :, lane_block(partner)], far_b.at[:, :, pl.ds(c * half, half)], 2 + c) for c in range(2)
    ]
    rest.append(load(pot_hbm.at[:, :, lane_block(pole)], v_ref, 4))
    rest.append(load(dx_hbm, dx_ref, 5))
    rest.append(load(dz_hbm, dz_ref, 6))
    rest.append(load(dy_hbm, dy_ref, 7))
    for copy in near:
        copy.wait()
    ysend[...] = jnp.swapaxes(own_b[...], 0, 1)
    pl.semaphore_wait(barrier, fy + poles * fz - 2)

    exchange(ysend, yb, 0, own_b, zb, 1)
    for copy in rest:
        copy.wait()

    def flat(ref):
        return ref[...].reshape(rows, nx)

    def column(ref, c):
        return ref[:, :, c * half : (c + 1) * half].reshape(-1, half)

    v = v_ref[...].reshape(rows, half)
    b = [column(own_b, c) for c in range(2)]
    s = []
    for c in range(2):
        whole = jnp.concatenate([b[c], column(far_b, c)], axis=1)
        s.append(v * b[c] + dot(whole, dx_ref[:, col0]))
        s_ref[:, :, c * half : (c + 1) * half] = s[c].reshape(cy, cz, half)
    acc1[0:1] = lanes(b[0] * b[0])
    acc1[1:2] = lanes(b[0] * b[1])
    acc1[2:3] = lanes(b[1] * b[1])
    acc1[5:8] = jnp.zeros((3, 128), jnp.float32)
    own = [lanes(b[c] * s[c]) for c in range(2)]

    arrived(zb, fz - 1, 1)
    zmul[...] = dot(dz_ref[...], flat(zb)).reshape(fz, cz, nx)
    for step in far_first(fz):
        push_z(zmul, zback, step, 3)
    zback[mz] = zmul[mz]
    arrived(yb, fy - 1, 0)
    ymul[...] = dot(dy_ref[...], flat(yb)).reshape(fy, cy, nx)
    for step in far_first(fy):
        push_y(ymul, yback, step, 2)
    yback[my] = ymul[my]

    both = lanes(flat(zb) * flat(zmul)) + lanes(flat(yb) * flat(ymul))
    acc1[3:4] = own[0] + both[:, col0]
    acc1[4:5] = own[1] + both[:, col1]
    spread(acc1, part1, fy, my, at_y, 6)

    arrived(zback, fz - 1, 3)
    s_ref[...] += zback[...]
    arrived(part1, fy - 1, 6)
    sum1[...] = jnp.sum(part1[...], axis=0)
    spread(sum1, part1z, poles * fz, plane, at_plane, 7)
    arrived(yback, fy - 1, 2)
    u_ref[...] = s_ref[...] + jnp.swapaxes(yback[...], 0, 1)
    yusend[...] = jnp.swapaxes(u_ref[...], 0, 1)
    exchange(yusend, yu, 4, u_ref, zu, 5)
    across = (partner, my, mz)
    push(u_ref.at[pl.ds(partner * split, split)], far_u, across, 10)
    push(u_ref.at[pl.ds(pole * split, split), :, lane_block(partner)], far_w, across, 11)

    arrived(part1z, poles * fz - 1, 7)
    total1 = jnp.sum(jnp.sum(part1z[...], axis=0), axis=1, keepdims=True)
    m00, m01, m11 = total1[0:1], total1[1:2], total1[2:3]
    mu = [total1[3:4] / m00, total1[4:5] / m11]

    w = [column(u_ref, c) - mu[c] * b[c] for c in range(2)]
    acc2[0:1] = lanes(w[0] * w[0])
    acc2[1:2] = lanes(w[0] * w[1])
    acc2[2:3] = lanes(w[1] * w[1])
    acc2[6:7] = lanes(b[0] * w[1])
    acc2[7:8] = lanes(b[1] * w[0])
    applied = [v * w[0], v * w[1]]
    terms = [lanes(w[0] * applied[0]), lanes(w[0] * applied[1]), lanes(w[1] * applied[1])]

    def quadratic(left, right):
        terms[0] += lanes(left[0] * right[0])
        terms[1] += lanes(left[0] * right[1])
        terms[2] += lanes(left[1] * right[1])

    arrived(far_u, split, 10)
    mine = pl.ds(pole * split, split)
    whole = []
    for c in range(2):
        block = slice(c * half, (c + 1) * half)
        near_part = u_ref[mine, :, block] - mu[c] * own_b[mine, :, block]
        far_part = far_u[:, :, block] - mu[c] * far_b[mine, :, block]
        whole.append(jnp.concatenate([near_part, far_part], axis=2).reshape(split * cz, nx))
    product = [dot(whole[c], dx_ref[...]) for c in range(2)]
    x_terms = [lanes(whole[0] * product[0]), lanes(whole[0] * product[1]), lanes(whole[1] * product[1])]
    for i in range(3):
        terms[i] = terms[i] + x_terms[i][:, col0] + x_terms[i][:, col1]

    def pencil(operator, u_pencil, b_pencil):
        left = [column(u_pencil, c) - mu[c] * column(b_pencil, c) for c in range(2)]
        quadratic(left, [dot(operator[...], left[c]) for c in range(2)])

    arrived(zu, fz - 1, 5)
    pencil(dz_ref, zu, zb)
    arrived(yu, fy - 1, 4)
    pencil(dy_ref, yu, yb)
    for i in range(3):
        acc2[3 + i : 4 + i] = terms[i]

    spread(acc2, part2, fy, my, at_y, 8)

    first = pole == 0
    my_mu = jnp.where(first, mu[0], mu[1])
    w_ref[0, :, :, lane_block(pole)] = jnp.where(first, w[0], w[1]).reshape(cy, cz, half)
    arrived(far_w, split, 11)
    others = pl.ds(partner * split, split)
    w_ref[0, mine, :, lane_block(partner)] = far_u[:, :, lane_block(pole)] - my_mu * far_b[mine, :, lane_block(pole)]
    w_ref[0, others, :, lane_block(partner)] = far_w[...] - my_mu * far_b[others, :, lane_block(pole)]

    arrived(part2, fy - 1, 8)
    sum2[...] = jnp.sum(part2[...], axis=0)
    spread(sum2, part2z, poles * fz, plane, at_plane, 9)

    sent(yb, fy - 1, 0)
    sent(zb, fz - 1, 1)
    sent(yback, fy - 1, 2)
    sent(zback, fz - 1, 3)
    sent(yu, fy - 1, 4)
    sent(zu, fz - 1, 5)
    sent(part1, fy - 1, 6)
    sent(part1z, poles * fz - 1, 7)
    sent(part2, fy - 1, 8)
    sent(far_u, split, 10)
    sent(far_w, split, 11)

    arrived(part2z, poles * fz - 1, 9)
    total2 = jnp.sum(jnp.sum(part2z[...], axis=0), axis=1, keepdims=True)
    w00, w01, w11, e00, e01, e11, c01, c10 = (total2[i : i + 1] for i in range(8))

    def factors(mean, norm, ww, whw):
        nu = jnp.where(ww > 0.0, whw / jnp.where(ww > 0.0, ww, 1.0), mean)
        t2 = ww / norm
        p, q = mean - 1.0, nu - 1.0
        trace, det = p + q, p * q - t2
        real, imag = det * det - 1.0, 2.0 * det - trace * trace
        size = real * real + imag * imag
        return ((det - q * trace) * imag - real) / size, trace * imag / size

    a0, f0 = factors(mu[0], m00, w00, e00)
    a1, f1 = factors(mu[1], m11, w11, e11)
    coef_ref[0:1] = jnp.broadcast_to(jnp.where(first, a0, a1), (1, 128))
    coef_ref[1:2] = jnp.broadcast_to(jnp.where(first, f0, f1), (1, 128))

    corr_ref[0:1, 0:1] = a0 * a0 * m00 + f0 * f0 * w00
    corr_ref[1:2, 1:2] = a1 * a1 * m11 + f1 * f1 * w11
    cross = a0 * a1 * m01 + a0 * f1 * c01 + f0 * a1 * c10 + f0 * f1 * w01
    corr_ref[0:1, 1:2] = cross
    corr_ref[1:2, 0:1] = cross
    energy_ref[0:1, 0:1] = a0 * a0 * mu[0] * m00 + 2.0 * a0 * f0 * w00 + f0 * f0 * e00
    energy_ref[1:2, 1:2] = a1 * a1 * mu[1] * m11 + 2.0 * a1 * f1 * w11 + f1 * f1 * e11
    cross = (
        a0 * a1 * (c01 + mu[1] * m01)
        + a0 * f1 * (w01 + mu[0] * c01)
        + f0 * a1 * (w01 + mu[1] * c10)
        + f0 * f1 * e01
    )
    energy_ref[0:1, 1:2] = cross
    energy_ref[1:2, 0:1] = cross
    sent(part2z, poles * fz - 1, 9)


def local(states, potential):
    columns, cy, cz, nx = states.shape
    fy, fz, poles = lax.axis_size("fy"), lax.axis_size("fz"), lax.axis_size("pole")
    half = nx // 2
    f32 = jnp.float32
    in_vmem = pl.BlockSpec(memory_space=pltpu.VMEM)
    in_hbm = pl.BlockSpec(memory_space=pl.ANY)

    def vmem(*shape):
        return pltpu.VMEM(shape, f32)

    x_block, y_block = vmem(cy, cz, nx), vmem(fy, cy, nx)
    sums = vmem(8, 128)
    w, coef, corr, energy = pl.pallas_call(
        functools.partial(kernel, cy, cz, nx, fy, fz, poles),
        out_shape=(
            jax.ShapeDtypeStruct((1, cy, cz, nx), f32),
            jax.ShapeDtypeStruct((8, 128), f32),
            jax.ShapeDtypeStruct((columns, columns), f32),
            jax.ShapeDtypeStruct((columns, columns), f32),
        ),
        in_specs=[in_hbm] * 5,
        out_specs=(in_vmem,) * 4,
        scratch_shapes=[
            x_block, x_block, vmem(cy, cz, half),
            vmem(nx, nx), vmem(cy * fy, cy * fy), vmem(cz * fz, cz * fz),
            x_block, x_block,
            y_block, y_block, vmem(fz, cz, nx),
            y_block, vmem(fz, cz, nx), y_block, vmem(fz, cz, nx),
            y_block, y_block, vmem(fz, cz, nx),
            vmem(cy // 2, cz, nx), vmem(cy // 2, cz, half),
            sums, sums, sums, sums,
            vmem(fy, 8, 128), vmem(fy, 8, 128), vmem(poles * fz, 8, 128), vmem(poles * fz, 8, 128),
            pltpu.SemaphoreType.DMA((8,)),
            pltpu.SemaphoreType.DMA((12,)),
            pltpu.SemaphoreType.DMA((12,)),
        ],
        compiler_params=pltpu.CompilerParams(
            collective_id=0, has_side_effects=True, vmem_limit_bytes=62 * 1024 * 1024
        ),
    )(
        states,
        potential,
        jnp.asarray(axis_operator(nx)),
        jnp.asarray(axis_operator(cy * fy)),
        jnp.asarray(axis_operator(cz * fz)),
    )
    mine = lax.dynamic_slice_in_dim(states, lax.axis_index("pole"), 1, 0)
    cells = 1.0 / float(nx * cy * fy * cz * fz)
    return coef[0, 0] * mine + coef[1, 0] * w, corr * cells, energy * cells


def solution(mesh):
    placed = (P(None, "fy", "fz", None), P("fy", "fz", None))
    return jax.shard_map(
        local,
        mesh=mesh,
        in_specs=placed,
        out_specs=(P("pole", "fy", "fz", None), P(), P()),
        check_vma=False,
    )
```

```python
import functools
import math

import jax
import jax.numpy as jnp
import numpy as np
from jax import lax
from jax.experimental import pallas as pl
from jax.experimental.pallas import tpu as pltpu
from jax.sharding import PartitionSpec as P

MESH = pl.DeviceIdType.MESH
HIGH = lax.Precision.HIGHEST


def axis_operator(length):
    index = np.arange(length)
    signed = np.where(index < length // 2, index, index - length) * (2.0 * math.pi / length)
    phases = (index[:, None] * index[None, :] % length) * (2.0 * math.pi / length)
    first = (np.cos(phases) @ (0.5 * signed * signed)) / length
    return np.asarray(first[(index[:, None] - index[None, :]) % length], np.float32)


def far_first(count):
    return sorted(range(1, count), key=lambda k: -min(k, count - k))


def dot(left, right):
    return jnp.dot(left, right, precision=HIGH, preferred_element_type=jnp.float32)


def lanes(product):
    return jnp.sum(product, axis=0, keepdims=True)


def kernel(
    cy, cz, nx, fy, fz, poles,
    states_hbm, pot_hbm, dx_hbm, dy_hbm, dz_hbm,
    out_ref, corr_ref, energy_ref,
    own_b, far_b, v_ref, dx_ref, dy_ref, dz_ref, s_ref, u_ref,
    ysend, yb, zb, ymul, zmul, yback, zback, yusend, yu, zu, far_u, far_w, w_ref,
    acc1, acc2, sum1, sum2, all1, all2, part1, part2, part1z, part2z,
    load_sem, send_sem, recv_sem,
):
    pole, my, mz = lax.axis_index("pole"), lax.axis_index("fy"), lax.axis_index("fz")
    partner = 1 - pole
    plane = pole * fz + mz
    rows = cy * cz
    half = nx // 2
    split = cy // 2
    col0, col1 = slice(0, half), slice(half, nx)

    def lane_block(index):
        return pl.ds(pl.multiple_of(index * half, half), half)

    def at_y(step):
        return (pole, lax.rem(my + step, fy), mz)

    def at_z(step):
        return (pole, my, lax.rem(mz + step, fz))

    def at_plane(step):
        other = lax.rem(plane + step, poles * fz)
        return (other // fz, my, lax.rem(other, fz))

    def push(src, dst, place, slot):
        pltpu.make_async_remote_copy(
            src_ref=src,
            dst_ref=dst,
            send_sem=send_sem.at[slot],
            recv_sem=recv_sem.at[slot],
            device_id=place,
            device_id_type=MESH,
        ).start()

    def push_y(src, dst, step, slot):
        push(src.at[lax.rem(my + step, fy)], dst.at[my], at_y(step), slot)

    def push_z(src, dst, step, slot):
        push(src.at[lax.rem(mz + step, fz)], dst.at[mz], at_z(step), slot)

    def exchange(ysrc, ydst, yslot, zsrc, zdst, zslot):
        ysteps, zsteps = far_first(fy), far_first(fz)
        for i in range(max(fy, fz) - 1):
            if i < len(ysteps):
                push_y(ysrc, ydst, ysteps[i], yslot)
            if i < len(zsteps):
                push_z(zsrc, zdst, zsteps[i], zslot)
        ydst[my] = ysrc[my]
        zdst[mz] = zsrc[mz]

    def spread(src, dst, count, me, place, slot):
        def body(step, carry):
            push(src, dst.at[me], place(step), slot)
            return carry

        lax.fori_loop(1, count, body, 0)
        dst[me] = src[...]

    def arrived(dst, count, slot):
        whole = dst.at[pl.ds(0, count)]
        pltpu.make_async_copy(whole, whole, recv_sem.at[slot]).wait()

    def sent(dst, count, slot):
        whole = dst.at[pl.ds(0, count)]
        pltpu.make_async_copy(whole, whole, send_sem.at[slot]).wait()

    def totals(parts, buffer, count):
        whole = jnp.sum(jnp.sum(parts[...], axis=0), axis=1, keepdims=True)
        buffer[...] = jnp.broadcast_to(whole, (8, 128))
        return [buffer[i : i + 1] for i in range(count)]

    barrier = pltpu.get_barrier_semaphore()

    for step in far_first(fy):
        pl.semaphore_signal(barrier, inc=1, device_id=at_y(step), device_id_type=MESH)
    for step in far_first(fz):
        pl.semaphore_signal(barrier, inc=1, device_id=at_z(step), device_id_type=MESH)
    across = (partner, my, mz)
    pl.semaphore_signal(barrier, inc=1, device_id=across, device_id_type=MESH)

    def load(src, dst, slot):
        copy = pltpu.make_async_copy(src, dst, load_sem.at[slot])
        copy.start()
        return copy

    near = [load(states_hbm.at[c, :, :, lane_block(pole)], own_b.at[:, :, pl.ds(c * half, half)], c) for c in range(2)]
    rest = [
        load(states_hbm.at[c, :, :, lane_block(partner)], far_b.at[:, :, pl.ds(c * half, half)], 2 + c) for c in range(2)
    ]
    rest.append(load(pot_hbm.at[:, :, lane_block(pole)], v_ref, 4))
    rest.append(load(dx_hbm, dx_ref, 5))
    rest.append(load(dz_hbm, dz_ref, 6))
    rest.append(load(dy_hbm, dy_ref, 7))
    for copy in near:
        copy.wait()
    ysend[...] = jnp.swapaxes(own_b[...], 0, 1)
    pl.semaphore_wait(barrier, fy + fz - 1)

    exchange(ysend, yb, 0, own_b, zb, 1)
    for copy in rest:
        copy.wait()

    def flat(ref):
        return ref[...].reshape(rows, nx)

    def column(ref, c):
        return ref[:, :, c * half : (c + 1) * half].reshape(-1, half)

    v = v_ref[...].reshape(rows, half)
    b = [column(own_b, c) for c in range(2)]
    s = []
    for c in range(2):
        whole = jnp.concatenate([b[c], column(far_b, c)], axis=1)
        s.append(v * b[c] + dot(whole, dx_ref[:, col0]))
        s_ref[:, :, c * half : (c + 1) * half] = s[c].reshape(cy, cz, half)
    acc1[0:1] = lanes(b[0] * b[0])
    acc1[1:2] = lanes(b[0] * b[1])
    acc1[2:3] = lanes(b[1] * b[1])
    acc1[5:8] = jnp.zeros((3, 128), jnp.float32)
    own = [lanes(b[c] * s[c]) for c in range(2)]

    arrived(zb, fz - 1, 1)
    zmul[...] = dot(dz_ref[...], flat(zb)).reshape(fz, cz, nx)
    for step in far_first(fz):
        push_z(zmul, zback, step, 3)
    zback[mz] = zmul[mz]
    arrived(yb, fy - 1, 0)
    ymul[...] = dot(dy_ref[...], flat(yb)).reshape(fy, cy, nx)
    for step in far_first(fy):
        push_y(ymul, yback, step, 2)
    yback[my] = ymul[my]

    both = lanes(flat(zb) * flat(zmul)) + lanes(flat(yb) * flat(ymul))
    acc1[3:4] = own[0] + both[:, col0]
    acc1[4:5] = own[1] + both[:, col1]
    spread(acc1, part1, fy, my, at_y, 6)

    arrived(zback, fz - 1, 3)
    s_ref[...] += zback[...]
    arrived(yback, fy - 1, 2)
    u_ref[...] = s_ref[...] + jnp.swapaxes(yback[...], 0, 1)
    yusend[...] = jnp.swapaxes(u_ref[...], 0, 1)
    push(u_ref.at[pl.ds(partner * split, split)], far_u, across, 10)
    exchange(yusend, yu, 4, u_ref, zu, 5)
    arrived(part1, fy - 1, 6)
    sum1[...] = jnp.sum(part1[...], axis=0)
    spread(sum1, part1z, poles * fz, plane, at_plane, 7)
    push(u_ref.at[pl.ds(pole * split, split), :, lane_block(partner)], far_w, across, 11)

    arrived(part1z, poles * fz - 1, 7)
    m00, m01, m11, h00, h11 = totals(part1z, all1, 5)
    mu = [h00 / m00, h11 / m11]

    w = [column(u_ref, c) - mu[c] * b[c] for c in range(2)]
    acc2[0:1] = lanes(w[0] * w[0])
    acc2[1:2] = lanes(w[0] * w[1])
    acc2[2:3] = lanes(w[1] * w[1])
    acc2[6:7] = lanes(b[0] * w[1])
    acc2[7:8] = lanes(b[1] * w[0])
    applied = [v * w[0], v * w[1]]
    terms = [lanes(w[0] * applied[0]), lanes(w[0] * applied[1]), lanes(w[1] * applied[1])]

    def quadratic(left, right):
        terms[0] += lanes(left[0] * right[0])
        terms[1] += lanes(left[0] * right[1])
        terms[2] += lanes(left[1] * right[1])

    arrived(far_u, split, 10)
    mine = pl.ds(pole * split, split)
    whole = []
    for c in range(2):
        block = slice(c * half, (c + 1) * half)
        near_part = u_ref[mine, :, block] - mu[c] * own_b[mine, :, block]
        far_part = far_u[:, :, block] - mu[c] * far_b[mine, :, block]
        whole.append(jnp.concatenate([near_part, far_part], axis=2).reshape(split * cz, nx))
    product = [dot(whole[c], dx_ref[...]) for c in range(2)]
    x_terms = [lanes(whole[0] * product[0]), lanes(whole[0] * product[1]), lanes(whole[1] * product[1])]
    for i in range(3):
        terms[i] = terms[i] + x_terms[i][:, col0] + x_terms[i][:, col1]

    def pencil(operator, u_pencil, b_pencil):
        left = [column(u_pencil, c) - mu[c] * column(b_pencil, c) for c in range(2)]
        quadratic(left, [dot(operator[...], left[c]) for c in range(2)])

    arrived(zu, fz - 1, 5)
    pencil(dz_ref, zu, zb)
    arrived(yu, fy - 1, 4)
    pencil(dy_ref, yu, yb)
    for i in range(3):
        acc2[3 + i : 4 + i] = terms[i]

    spread(acc2, part2, fy, my, at_y, 8)

    first = pole == 0
    my_mu = jnp.where(first, mu[0], mu[1])
    w_ref[:, :, lane_block(pole)] = jnp.where(first, w[0], w[1]).reshape(cy, cz, half)
    arrived(far_w, split, 11)
    others = pl.ds(partner * split, split)
    w_ref[mine, :, lane_block(partner)] = far_u[:, :, lane_block(pole)] - my_mu * far_b[mine, :, lane_block(pole)]
    w_ref[others, :, lane_block(partner)] = far_w[...] - my_mu * far_b[others, :, lane_block(pole)]

    arrived(part2, fy - 1, 8)
    sum2[...] = jnp.sum(part2[...], axis=0)
    spread(sum2, part2z, poles * fz, plane, at_plane, 9)

    sent(yb, fy - 1, 0)
    sent(zb, fz - 1, 1)
    sent(yback, fy - 1, 2)
    sent(zback, fz - 1, 3)
    sent(yu, fy - 1, 4)
    sent(zu, fz - 1, 5)
    sent(part1, fy - 1, 6)
    sent(part1z, poles * fz - 1, 7)
    sent(part2, fy - 1, 8)
    sent(far_u, split, 10)
    sent(far_w, split, 11)

    arrived(part2z, poles * fz - 1, 9)
    w00, w01, w11, e00, e01, e11, c01, c10 = totals(part2z, all2, 8)

    def factors(mean, norm, ww, whw):
        nu = jnp.where(ww > 0.0, whw / jnp.where(ww > 0.0, ww, 1.0), mean)
        t2 = ww / norm
        p, q = mean - 1.0, nu - 1.0
        trace, det = p + q, p * q - t2
        real, imag = det * det - 1.0, 2.0 * det - trace * trace
        size = real * real + imag * imag
        return ((det - q * trace) * imag - real) / size, trace * imag / size

    def gram(ref, upper, cross, lower):
        lane = lax.broadcasted_iota(jnp.int32, (1, 128), 1)
        ref[0:1, :] = jnp.where(lane == 0, upper, cross)[:, 0:2]
        ref[1:2, :] = jnp.where(lane == 0, cross, lower)[:, 0:2]

    a0, f0 = factors(mu[0], m00, w00, e00)
    a1, f1 = factors(mu[1], m11, w11, e11)
    a, f = jnp.where(first, a0, a1), jnp.where(first, f0, f1)
    for block, base in ((lane_block(pole), own_b), (lane_block(partner), far_b)):
        out_ref[0, :, :, block] = a * base[:, :, lane_block(pole)] + f * w_ref[:, :, block]

    cross = a0 * a1 * m01 + a0 * f1 * c01 + f0 * a1 * c10 + f0 * f1 * w01
    gram(corr_ref, a0 * a0 * m00 + f0 * f0 * w00, cross, a1 * a1 * m11 + f1 * f1 * w11)
    cross = (
        a0 * a1 * (c01 + mu[1] * m01)
        + a0 * f1 * (w01 + mu[0] * c01)
        + f0 * a1 * (w01 + mu[1] * c10)
        + f0 * f1 * e01
    )
    gram(
        energy_ref,
        a0 * a0 * mu[0] * m00 + 2.0 * a0 * f0 * w00 + f0 * f0 * e00,
        cross,
        a1 * a1 * mu[1] * m11 + 2.0 * a1 * f1 * w11 + f1 * f1 * e11,
    )
    sent(part2z, poles * fz - 1, 9)


def local(states, potential):
    columns, cy, cz, nx = states.shape
    fy, fz, poles = lax.axis_size("fy"), lax.axis_size("fz"), lax.axis_size("pole")
    half = nx // 2
    f32 = jnp.float32
    in_vmem = pl.BlockSpec(memory_space=pltpu.VMEM)
    in_hbm = pl.BlockSpec(memory_space=pl.ANY)

    def vmem(*shape):
        return pltpu.VMEM(shape, f32)

    x_block, y_block = vmem(cy, cz, nx), vmem(fy, cy, nx)
    sums = vmem(8, 128)
    filtered, corr, energy = pl.pallas_call(
        functools.partial(kernel, cy, cz, nx, fy, fz, poles),
        out_shape=(
            jax.ShapeDtypeStruct((1, cy, cz, nx), f32),
            jax.ShapeDtypeStruct((columns, columns), f32),
            jax.ShapeDtypeStruct((columns, columns), f32),
        ),
        in_specs=[in_hbm] * 5,
        out_specs=(in_vmem,) * 3,
        scratch_shapes=[
            x_block, x_block, vmem(cy, cz, half),
            vmem(nx, nx), vmem(cy * fy, cy * fy), vmem(cz * fz, cz * fz),
            x_block, x_block,
            y_block, y_block, vmem(fz, cz, nx),
            y_block, vmem(fz, cz, nx), y_block, vmem(fz, cz, nx),
            y_block, y_block, vmem(fz, cz, nx),
            vmem(cy // 2, cz, nx), vmem(cy // 2, cz, half), x_block,
            sums, sums, sums, sums, sums, sums,
            vmem(fy, 8, 128), vmem(fy, 8, 128), vmem(poles * fz, 8, 128), vmem(poles * fz, 8, 128),
            pltpu.SemaphoreType.DMA((8,)),
            pltpu.SemaphoreType.DMA((12,)),
            pltpu.SemaphoreType.DMA((12,)),
        ],
        compiler_params=pltpu.CompilerParams(
            collective_id=0, has_side_effects=True, vmem_limit_bytes=32 * 1024 * 1024
        ),
    )(
        *(
            pltpu.with_memory_space_constraint(operand, pltpu.HBM)
            for operand in (
                states,
                potential,
                jnp.asarray(axis_operator(nx)),
                jnp.asarray(axis_operator(cy * fy)),
                jnp.asarray(axis_operator(cz * fz)),
            )
        )
    )
    cells = 1.0 / float(nx * cy * fy * cz * fz)
    return filtered, corr * cells, energy * cells


def solution(mesh):
    placed = (P(None, "fy", "fz", None), P("fy", "fz", None))
    return jax.shard_map(
        local,
        mesh=mesh,
        in_specs=placed,
        out_specs=(P("pole", "fy", "fz", None), P(), P()),
        check_vma=False,
    )
```

```python
import functools
import math

import jax
import jax.numpy as jnp
import numpy as np
from jax import lax
from jax.experimental import pallas as pl
from jax.experimental.pallas import tpu as pltpu
from jax.sharding import PartitionSpec as P

MESH = pl.DeviceIdType.MESH
HIGH = lax.Precision.HIGHEST


def axis_operator(length):
    index = np.arange(length)
    signed = np.where(index < length // 2, index, index - length) * (2.0 * math.pi / length)
    phases = (index[:, None] * index[None, :] % length) * (2.0 * math.pi / length)
    first = (np.cos(phases) @ (0.5 * signed * signed)) / length
    return np.asarray(first[(index[:, None] - index[None, :]) % length], np.float32)


def far_first(count):
    return sorted(range(1, count), key=lambda k: -min(k, count - k))


def dot(left, right):
    return jnp.dot(left, right, precision=HIGH, preferred_element_type=jnp.float32)


def lanes(product):
    return jnp.sum(product, axis=0, keepdims=True)


def kernel(
    cy, cz, nx, fy, fz, poles,
    states_hbm, pot_hbm, dx_hbm, dy_hbm, dz_hbm,
    out_ref, corr_ref, energy_ref,
    own_b, far_b, v_ref, dx_ref, dy_ref, dz_ref, s_ref, u_ref,
    ysend, yb, zb, ymul, zmul, yback, zback, yusend, yu, zu, far_u, far_w, u_far, whole_u,
    acc, sum_y, part_y, part_z, all_sums, lane_sums, cancelled,
    load_sem, send_sem, recv_sem,
):
    pole, my, mz = lax.axis_index("pole"), lax.axis_index("fy"), lax.axis_index("fz")
    partner = 1 - pole
    plane = pole * fz + mz
    rows = cy * cz
    half = nx // 2
    split = cy // 2
    col0, col1 = slice(0, half), slice(half, nx)

    def lane_block(index):
        return pl.ds(pl.multiple_of(index * half, half), half)

    def at_y(step):
        return (pole, lax.rem(my + step, fy), mz)

    def at_z(step):
        return (pole, my, lax.rem(mz + step, fz))

    def at_plane(step):
        other = lax.rem(plane + step, poles * fz)
        return (other // fz, my, lax.rem(other, fz))

    def push(src, dst, place, slot):
        pltpu.make_async_remote_copy(
            src_ref=src,
            dst_ref=dst,
            send_sem=send_sem.at[slot],
            recv_sem=recv_sem.at[slot],
            device_id=place,
            device_id_type=MESH,
        ).start()

    def push_y(src, dst, step, slot):
        push(src.at[lax.rem(my + step, fy)], dst.at[my], at_y(step), slot)

    def push_z(src, dst, step, slot):
        push(src.at[lax.rem(mz + step, fz)], dst.at[mz], at_z(step), slot)

    def exchange(ysrc, ydst, yslot, zsrc, zdst, zslot):
        ysteps, zsteps = far_first(fy), far_first(fz)
        for i in range(max(fy, fz) - 1):
            if i < len(ysteps):
                push_y(ysrc, ydst, ysteps[i], yslot)
            if i < len(zsteps):
                push_z(zsrc, zdst, zsteps[i], zslot)
        ydst[my] = ysrc[my]
        zdst[mz] = zsrc[mz]

    def spread(src, dst, count, me, place, slot):
        def body(step, carry):
            push(src, dst.at[me], place(step), slot)
            return carry

        lax.fori_loop(1, count, body, 0)
        dst[me] = src[...]

    def arrived(dst, count, slot):
        whole = dst.at[pl.ds(0, count)]
        pltpu.make_async_copy(whole, whole, recv_sem.at[slot]).wait()

    def sent(dst, count, slot):
        whole = dst.at[pl.ds(0, count)]
        pltpu.make_async_copy(whole, whole, send_sem.at[slot]).wait()

    barrier = pltpu.get_barrier_semaphore()

    for step in far_first(fy):
        pl.semaphore_signal(barrier, inc=1, device_id=at_y(step), device_id_type=MESH)
    for step in far_first(fz):
        pl.semaphore_signal(barrier, inc=1, device_id=at_z(step), device_id_type=MESH)
    across = (partner, my, mz)
    pl.semaphore_signal(barrier, inc=1, device_id=across, device_id_type=MESH)

    def load(src, dst, slot):
        copy = pltpu.make_async_copy(src, dst, load_sem.at[slot])
        copy.start()
        return copy

    near = [load(states_hbm.at[c, :, :, lane_block(pole)], own_b.at[:, :, pl.ds(c * half, half)], c) for c in range(2)]
    rest = [
        load(states_hbm.at[c, :, :, lane_block(partner)], far_b.at[:, :, pl.ds(c * half, half)], 2 + c) for c in range(2)
    ]
    rest.append(load(pot_hbm.at[:, :, lane_block(pole)], v_ref, 4))
    rest.append(load(dx_hbm, dx_ref, 5))
    rest.append(load(dz_hbm, dz_ref, 6))
    rest.append(load(dy_hbm, dy_ref, 7))
    for copy in near:
        copy.wait()
    ysend[...] = jnp.swapaxes(own_b[...], 0, 1)
    pl.semaphore_wait(barrier, fy + fz - 1)

    exchange(ysend, yb, 0, own_b, zb, 1)
    for copy in rest:
        copy.wait()

    def flat(ref):
        return ref[...].reshape(rows, nx)

    def column(ref, c):
        return ref[:, :, c * half : (c + 1) * half].reshape(-1, half)

    v = v_ref[...].reshape(rows, half)
    b = [column(own_b, c) for c in range(2)]
    s = []
    for c in range(2):
        whole = jnp.concatenate([b[c], column(far_b, c)], axis=1)
        s.append(v * b[c] + dot(whole, dx_ref[:, col0]))
        s_ref[:, :, c * half : (c + 1) * half] = s[c].reshape(cy, cz, half)
    acc[0:1] = lanes(b[0] * b[0])
    acc[1:2] = lanes(b[0] * b[1])
    acc[2:3] = lanes(b[1] * b[1])
    acc[12:16] = jnp.zeros((4, 128), jnp.float32)

    arrived(zb, fz - 1, 1)
    zmul[...] = dot(dz_ref[...], flat(zb)).reshape(fz, cz, nx)
    for step in far_first(fz):
        push_z(zmul, zback, step, 3)
    zback[mz] = zmul[mz]
    arrived(yb, fy - 1, 0)
    ymul[...] = dot(dy_ref[...], flat(yb)).reshape(fy, cy, nx)
    for step in far_first(fy):
        push_y(ymul, yback, step, 2)
    yback[my] = ymul[my]

    arrived(zback, fz - 1, 3)
    s_ref[...] += zback[...]
    arrived(yback, fy - 1, 2)
    u_ref[...] = s_ref[...] + jnp.swapaxes(yback[...], 0, 1)
    yusend[...] = jnp.swapaxes(u_ref[...], 0, 1)
    push(u_ref.at[pl.ds(partner * split, split)], far_u, across, 6)
    exchange(yusend, yu, 4, u_ref, zu, 5)
    push(u_ref.at[pl.ds(pole * split, split), :, lane_block(partner)], far_w, across, 7)

    u = [column(u_ref, c) for c in range(2)]
    acc[3:4] = lanes(b[0] * u[0])
    acc[4:5] = lanes(b[0] * u[1])
    acc[5:6] = lanes(b[1] * u[1])
    acc[6:7] = lanes(u[0] * u[0])
    acc[7:8] = lanes(u[0] * u[1])
    acc[8:9] = lanes(u[1] * u[1])
    applied = [v * u[0], v * u[1]]
    terms = [lanes(u[0] * applied[0]), lanes(u[0] * applied[1]), lanes(u[1] * applied[1])]

    def quadratic(left, right):
        terms[0] += lanes(left[0] * right[0])
        terms[1] += lanes(left[0] * right[1])
        terms[2] += lanes(left[1] * right[1])

    arrived(far_u, split, 6)
    mine, others = pl.ds(pole * split, split), pl.ds(partner * split, split)
    for c in range(2):
        block = slice(c * half, (c + 1) * half)
        whole_u[c] = jnp.concatenate([u_ref[mine, :, block], far_u[:, :, block]], axis=2).reshape(split * cz, nx)
    whole = [whole_u[0], whole_u[1]]
    product = [dot(whole[c], dx_ref[...]) for c in range(2)]
    for part in (col0, col1):
        quadratic([left[:, part] for left in whole], [right[:, part] for right in product])

    def pencil(operator, u_pencil):
        product = dot(operator[...], flat(u_pencil))
        left = flat(u_pencil)
        quadratic([left[:, col0], left[:, col1]], [product[:, col0], product[:, col1]])

    arrived(zu, fz - 1, 5)
    pencil(dz_ref, zu)
    arrived(yu, fy - 1, 4)
    pencil(dy_ref, yu)
    for i in range(3):
        acc[9 + i : 10 + i] = terms[i]

    spread(acc, part_y, fy, my, at_y, 8)

    first = pole == 0
    arrived(far_w, split, 7)
    u_far[mine] = far_u[:, :, lane_block(pole)]
    u_far[others] = far_w[...]

    arrived(part_y, fy - 1, 8)
    sum_y[...] = jnp.sum(part_y[...], axis=0)
    spread(sum_y, part_z, poles * fz, plane, at_plane, 9)

    sent(yb, fy - 1, 0)
    sent(zb, fz - 1, 1)
    sent(yback, fy - 1, 2)
    sent(zback, fz - 1, 3)
    sent(yu, fy - 1, 4)
    sent(zu, fz - 1, 5)
    sent(far_u, split, 6)
    sent(far_w, split, 7)
    sent(part_y, fy - 1, 8)

    arrived(part_z, poles * fz - 1, 9)
    by_lane = jnp.sum(part_z[...], axis=0)

    def totals(value, buffer):
        buffer[...] = jnp.broadcast_to(jnp.sum(value, axis=1, keepdims=True), value.shape)
        return [buffer[i : i + 1] for i in range(value.shape[0])]

    m00, m01, m11, h00, _, h11 = totals(by_lane, all_sums)[:6]
    mu = [h00 / m00, h11 / m11]
    lane_sums[...] = by_lane
    l00, l01, l11, b00, b01, b11, u00, u01, u11, e00, e01, e11 = (lane_sums[i : i + 1] for i in range(12))
    cancelled[0:1] = u00 - mu[0] * (2.0 * b00 - mu[0] * l00)
    cancelled[1:2] = u01 - (mu[0] + mu[1]) * b01 + mu[0] * mu[1] * l01
    cancelled[2:3] = u11 - mu[1] * (2.0 * b11 - mu[1] * l11)
    cancelled[3:4] = e00 - mu[0] * (2.0 * u00 - mu[0] * b00)
    cancelled[4:5] = e01 - (mu[0] + mu[1]) * u01 + mu[0] * mu[1] * b01
    cancelled[5:6] = e11 - mu[1] * (2.0 * u11 - mu[1] * b11)
    cancelled[6:7] = b01 - mu[1] * l01
    cancelled[7:8] = b01 - mu[0] * l01
    w00, w01, w11, e00, e01, e11, c01, c10 = totals(cancelled[...], cancelled)

    top = 1.5 * math.pi**2 + 3.0

    def factors(mean, norm, ww, whw):
        nu = jnp.where(ww > 0.0, jnp.clip(whw / jnp.where(ww > 0.0, ww, 1.0), 0.0, top), mean)
        t2 = jnp.maximum(ww, 0.0) / norm
        p, q = mean - 1.0, nu - 1.0
        trace, det = p + q, p * q - t2
        real, imag = det * det - 1.0, 2.0 * det - trace * trace
        size = real * real + imag * imag
        return ((det - q * trace) * imag - real) / size, trace * imag / size

    def gram(ref, upper, cross, lower):
        lane = lax.broadcasted_iota(jnp.int32, (1, 128), 1)
        ref[0:1, :] = jnp.where(lane == 0, upper, cross)[:, 0:2]
        ref[1:2, :] = jnp.where(lane == 0, cross, lower)[:, 0:2]

    a0, f0 = factors(mu[0], m00, w00, e00)
    a1, f1 = factors(mu[1], m11, w11, e11)
    a, f = jnp.where(first, a0, a1), jnp.where(first, f0, f1)
    my_mu = jnp.where(first, mu[0], mu[1])
    column_block = lane_block(pole)
    for block, base, applied in (
        (lane_block(pole), own_b[:, :, column_block], u_ref[:, :, column_block]),
        (lane_block(partner), far_b[:, :, column_block], u_far[...]),
    ):
        out_ref[0, :, :, block] = a * base + f * (applied - my_mu * base)
    cross = a0 * a1 * m01 + a0 * f1 * c01 + f0 * a1 * c10 + f0 * f1 * w01
    gram(corr_ref, a0 * a0 * m00 + f0 * f0 * w00, cross, a1 * a1 * m11 + f1 * f1 * w11)
    cross = (
        a0 * a1 * (c01 + mu[1] * m01)
        + a0 * f1 * (w01 + mu[0] * c01)
        + f0 * a1 * (w01 + mu[1] * c10)
        + f0 * f1 * e01
    )
    gram(
        energy_ref,
        a0 * a0 * mu[0] * m00 + 2.0 * a0 * f0 * w00 + f0 * f0 * e00,
        cross,
        a1 * a1 * mu[1] * m11 + 2.0 * a1 * f1 * w11 + f1 * f1 * e11,
    )
    sent(part_z, poles * fz - 1, 9)


def local(states, potential):
    columns, cy, cz, nx = states.shape
    fy, fz, poles = lax.axis_size("fy"), lax.axis_size("fz"), lax.axis_size("pole")
    half = nx // 2
    f32 = jnp.float32
    in_vmem = pl.BlockSpec(memory_space=pltpu.VMEM)
    in_hbm = pl.BlockSpec(memory_space=pl.ANY)

    def vmem(*shape):
        return pltpu.VMEM(shape, f32)

    x_block, y_block = vmem(cy, cz, nx), vmem(fy, cy, nx)
    sums = vmem(16, 128)
    filtered, corr, energy = pl.pallas_call(
        functools.partial(kernel, cy, cz, nx, fy, fz, poles),
        out_shape=(
            jax.ShapeDtypeStruct((1, cy, cz, nx), f32),
            jax.ShapeDtypeStruct((columns, columns), f32),
            jax.ShapeDtypeStruct((columns, columns), f32),
        ),
        in_specs=[in_hbm] * 5,
        out_specs=(in_vmem,) * 3,
        scratch_shapes=[
            x_block, x_block, vmem(cy, cz, half),
            vmem(nx, nx), vmem(cy * fy, cy * fy), vmem(cz * fz, cz * fz),
            x_block, x_block,
            y_block, y_block, vmem(fz, cz, nx),
            y_block, vmem(fz, cz, nx), y_block, vmem(fz, cz, nx),
            y_block, y_block, vmem(fz, cz, nx),
            vmem(cy // 2, cz, nx), vmem(cy // 2, cz, half), vmem(cy, cz, half), vmem(columns, cy // 2 * cz, nx),
            sums, sums, vmem(fy, 16, 128), vmem(poles * fz, 16, 128), sums, sums, vmem(8, 128),
            pltpu.SemaphoreType.DMA((8,)),
            pltpu.SemaphoreType.DMA((10,)),
            pltpu.SemaphoreType.DMA((10,)),
        ],
        compiler_params=pltpu.CompilerParams(
            collective_id=0, has_side_effects=True, vmem_limit_bytes=32 * 1024 * 1024
        ),
    )(
        *(
            pltpu.with_memory_space_constraint(operand, pltpu.HBM)
            for operand in (
                states,
                potential,
                jnp.asarray(axis_operator(nx)),
                jnp.asarray(axis_operator(cy * fy)),
                jnp.asarray(axis_operator(cz * fz)),
            )
        )
    )
    cells = 1.0 / float(nx * cy * fy * cz * fz)
    return filtered, corr * cells, energy * cells


def solution(mesh):
    placed = (P(None, "fy", "fz", None), P("fy", "fz", None))
    return jax.shard_map(
        local,
        mesh=mesh,
        in_specs=placed,
        out_specs=(P("pole", "fy", "fz", None), P(), P()),
        check_vma=False,
    )
```

```python
import functools
import math

import jax
import jax.numpy as jnp
import numpy as np
from jax import lax
from jax.experimental import pallas as pl
from jax.experimental.pallas import tpu as pltpu
from jax.sharding import PartitionSpec as P

MESH = pl.DeviceIdType.MESH
HIGH = lax.Precision.HIGHEST


def axis_operator(length):
    index = np.arange(length)
    signed = np.where(index < length // 2, index, index - length) * (2.0 * math.pi / length)
    phases = (index[:, None] * index[None, :] % length) * (2.0 * math.pi / length)
    first = (np.cos(phases) @ (0.5 * signed * signed)) / length
    return np.asarray(first[(index[:, None] - index[None, :]) % length], np.float32)


def far_first(count):
    return sorted(range(1, count), key=lambda k: -min(k, count - k))


def dot(left, right):
    return jnp.dot(left, right, precision=HIGH, preferred_element_type=jnp.float32)


def lanes(product):
    return jnp.sum(product, axis=0, keepdims=True)


def kernel(
    cy, cz, nx, fy, fz, poles,
    states_hbm, pot_hbm, dx_hbm, dy_hbm, dz_hbm,
    out_ref, corr_ref, energy_ref,
    own_b, far_b, v_ref, dx_ref, dy_ref, dz_ref, s_ref, u_ref,
    ysend, yb, zb, ymul, zmul, yback, zback, yusend, yu, zu, far_u, far_w, u_far, whole_u,
    acc, mine_sums, core_sums, chip_sums, parts, rows_ref,
    load_sem, send_sem, recv_sem,
):
    pole, my, mz = lax.axis_index("pole"), lax.axis_index("fy"), lax.axis_index("fz")
    partner = 1 - pole
    plane = pole * fz + mz
    rows = cy * cz
    half = nx // 2
    split = cy // 2
    col0, col1 = slice(0, half), slice(half, nx)

    def lane_block(index):
        return pl.ds(pl.multiple_of(index * half, half), half)

    def at_y(step):
        return (pole, lax.rem(my + step, fy), mz)

    def at_z(step):
        return (pole, my, lax.rem(mz + step, fz))

    def at_plane(step):
        other = lax.rem(plane + step, poles * fz)
        return (other // fz, my, lax.rem(other, fz))

    def push(src, dst, place, slot):
        pltpu.make_async_remote_copy(
            src_ref=src,
            dst_ref=dst,
            send_sem=send_sem.at[slot],
            recv_sem=recv_sem.at[slot],
            device_id=place,
            device_id_type=MESH,
        ).start()

    def push_y(src, dst, step, slot):
        push(src.at[lax.rem(my + step, fy)], dst.at[my], at_y(step), slot)

    def push_z(src, dst, step, slot):
        push(src.at[lax.rem(mz + step, fz)], dst.at[mz], at_z(step), slot)

    def scatter_y(src, dst, slot):
        for step in far_first(fy):
            push_y(src, dst, step, slot)
        dst[my] = src[my]

    def scatter_z(src, dst, slot):
        for step in far_first(fz):
            push_z(src, dst, step, slot)
        dst[mz] = src[mz]

    def arrived(dst, count, slot):
        whole = dst.at[pl.ds(0, count)]
        pltpu.make_async_copy(whole, whole, recv_sem.at[slot]).wait()

    def sent(dst, count, slot):
        whole = dst.at[pl.ds(0, count)]
        pltpu.make_async_copy(whole, whole, send_sem.at[slot]).wait()

    barrier = pltpu.get_barrier_semaphore()

    for step in far_first(fy):
        pl.semaphore_signal(barrier, inc=1, device_id=at_y(step), device_id_type=MESH)
    for step in far_first(fz):
        pl.semaphore_signal(barrier, inc=1, device_id=at_z(step), device_id_type=MESH)
    across = (partner, my, mz)
    pl.semaphore_signal(barrier, inc=1, device_id=across, device_id_type=MESH)

    def load(src, dst, slot):
        copy = pltpu.make_async_copy(src, dst, load_sem.at[slot])
        copy.start()
        return copy

    near = [load(states_hbm.at[c, :, :, lane_block(pole)], own_b.at[:, :, pl.ds(c * half, half)], c) for c in range(2)]
    rest = [
        load(states_hbm.at[c, :, :, lane_block(partner)], far_b.at[:, :, pl.ds(c * half, half)], 2 + c) for c in range(2)
    ]
    rest.append(load(pot_hbm.at[:, :, lane_block(pole)], v_ref, 4))
    rest.append(load(dx_hbm, dx_ref, 5))
    rest.append(load(dz_hbm, dz_ref, 6))
    rest.append(load(dy_hbm, dy_ref, 7))
    for copy in near:
        copy.wait()
    ysend[...] = jnp.swapaxes(own_b[...], 0, 1)
    pl.semaphore_wait(barrier, fy + fz - 1)

    scatter_y(ysend, yb, 0)
    scatter_z(own_b, zb, 1)
    for copy in rest:
        copy.wait()

    def flat(ref):
        return ref[...].reshape(rows, nx)

    def column(ref, c):
        return ref[:, :, c * half : (c + 1) * half].reshape(-1, half)

    v = v_ref[...].reshape(rows, half)
    b = [column(own_b, c) for c in range(2)]
    s = []
    for c in range(2):
        whole = jnp.concatenate([b[c], column(far_b, c)], axis=1)
        s.append(v * b[c] + dot(whole, dx_ref[:, col0]))
        s_ref[:, :, c * half : (c + 1) * half] = s[c].reshape(cy, cz, half)
    acc[0:1] = lanes(b[0] * b[0])
    acc[1:2] = lanes(b[0] * b[1])
    acc[2:3] = lanes(b[1] * b[1])
    acc[12:16] = jnp.zeros((4, 128), jnp.float32)

    arrived(zb, fz - 1, 1)
    zmul[...] = dot(dz_ref[...], flat(zb)).reshape(fz, cz, nx)
    scatter_z(zmul, zback, 3)
    arrived(yb, fy - 1, 0)
    ymul[...] = dot(dy_ref[...], flat(yb)).reshape(fy, cy, nx)
    scatter_y(ymul, yback, 2)

    arrived(zback, fz - 1, 3)
    yusend[...] = jnp.swapaxes(s_ref[...] + zback[...], 0, 1)
    arrived(yback, fy - 1, 2)
    yusend[...] += yback[...]
    scatter_y(yusend, yu, 4)
    u_ref[...] = jnp.swapaxes(yusend[...], 0, 1)
    push(u_ref.at[pl.ds(partner * split, split)], far_u, across, 6)
    scatter_z(u_ref, zu, 5)
    push(u_ref.at[pl.ds(pole * split, split), :, lane_block(partner)], far_w, across, 7)

    u = [column(u_ref, c) for c in range(2)]
    acc[3:4] = lanes(b[0] * u[0])
    acc[4:5] = lanes(b[0] * u[1])
    acc[5:6] = lanes(b[1] * u[1])
    acc[6:7] = lanes(u[0] * u[0])
    acc[7:8] = lanes(u[0] * u[1])
    acc[8:9] = lanes(u[1] * u[1])
    applied = [v * u[0], v * u[1]]
    terms = [lanes(u[0] * applied[0]), lanes(u[0] * applied[1]), lanes(u[1] * applied[1])]

    def quadratic(left, right):
        terms[0] += lanes(left[0] * right[0])
        terms[1] += lanes(left[0] * right[1])
        terms[2] += lanes(left[1] * right[1])

    arrived(far_u, split, 6)
    mine, others = pl.ds(pole * split, split), pl.ds(partner * split, split)
    for c in range(2):
        block = slice(c * half, (c + 1) * half)
        whole_u[c] = jnp.concatenate([u_ref[mine, :, block], far_u[:, :, block]], axis=2).reshape(split * cz, nx)
    whole = [whole_u[0], whole_u[1]]
    product = [dot(whole[c], dx_ref[...]) for c in range(2)]
    for part in (col0, col1):
        quadratic([left[:, part] for left in whole], [right[:, part] for right in product])

    def pencil(operator, u_pencil):
        product = dot(operator[...], flat(u_pencil))
        left = flat(u_pencil)
        quadratic([left[:, col0], left[:, col1]], [product[:, col0], product[:, col1]])

    arrived(zu, fz - 1, 5)
    pencil(dz_ref, zu)
    arrived(yu, fy - 1, 4)
    pencil(dy_ref, yu)
    for i in range(3):
        acc[9 + i : 10 + i] = terms[i]

    lane = lax.broadcasted_iota(jnp.int32, (16, 128), 1)
    row = lax.broadcasted_iota(jnp.int32, (16, 128), 0)
    folded = acc[...]
    for shift in (64, 32, 16, 8):
        folded = folded + pltpu.roll(folded, shift, 1)
    mine_sums[...] = jnp.sum(jnp.where(lane // 8 == row, folded, 0.0), axis=0, keepdims=True)
    push(mine_sums, core_sums, (pole, my, mz + 1 - 2 * lax.rem(mz, 2)), 8)

    first = pole == 0
    arrived(far_w, split, 7)
    u_far[mine] = far_u[:, :, lane_block(pole)]
    u_far[others] = far_w[...]

    whole_core = core_sums.at[pl.ds(0, 1)]
    pltpu.make_async_copy(whole_core, whole_core, recv_sem.at[8]).wait()
    chips = poles * fz // 2
    chip = my * chips + plane // 2
    chip_sums[...] = mine_sums[...] + core_sums[...]
    for step_y in far_first(fy) + [0]:

        def body(step, carry, step_y=step_y):
            other = lax.rem(plane + 2 * step, 2 * chips)
            place = (other // fz, lax.rem(my + step_y, fy), lax.rem(other, fz))
            push(chip_sums, parts.at[chip], place, 9)
            return carry

        lax.fori_loop(0 if step_y else 1, chips, body, 0)
    parts[chip] = chip_sums[...]

    sent(yb, fy - 1, 0)
    sent(zb, fz - 1, 1)
    sent(yback, fy - 1, 2)
    sent(zback, fz - 1, 3)
    sent(yu, fy - 1, 4)
    sent(zu, fz - 1, 5)
    sent(far_u, split, 6)
    sent(far_w, split, 7)
    pltpu.make_async_copy(whole_core, whole_core, send_sem.at[8]).wait()

    arrived(parts, fy * chips - 1, 9)
    total = jnp.sum(parts[...], axis=0)
    slim = lax.broadcasted_iota(jnp.int32, (8, 128), 1) < 8

    def totals(values):
        for i, value in enumerate(values):
            rows_ref[i : i + 1] = value
        summed = jnp.sum(jnp.where(slim, rows_ref[...], 0.0), axis=1, keepdims=True)
        rows_ref[...] = jnp.broadcast_to(summed, (8, 128))
        return [rows_ref[i : i + 1] for i in range(len(values))]

    l00, l01, l11, b00, b01, b11, u00, u01, u11, e00, e01, e11 = (
        pltpu.roll(total, (128 - 8 * i) % 128, 1) if i else total for i in range(12)
    )
    m00, m01, m11, h00, h11 = totals([l00, l01, l11, b00, b11])
    mu = [h00 / m00, h11 / m11]
    w00, w01, w11, e00, e01, e11, c01, c10 = totals(
        [
            u00 - mu[0] * (2.0 * b00 - mu[0] * l00),
            u01 - (mu[0] + mu[1]) * b01 + mu[0] * mu[1] * l01,
            u11 - mu[1] * (2.0 * b11 - mu[1] * l11),
            e00 - mu[0] * (2.0 * u00 - mu[0] * b00),
            e01 - (mu[0] + mu[1]) * u01 + mu[0] * mu[1] * b01,
            e11 - mu[1] * (2.0 * u11 - mu[1] * b11),
            b01 - mu[1] * l01,
            b01 - mu[0] * l01,
        ]
    )

    top = 1.5 * math.pi**2 + 3.0

    def factors(mean, norm, ww, whw):
        nu = jnp.where(ww > 0.0, jnp.clip(whw / jnp.where(ww > 0.0, ww, 1.0), 0.0, top), mean)
        t2 = jnp.maximum(ww, 0.0) / norm
        p, q = mean - 1.0, nu - 1.0
        trace, det = p + q, p * q - t2
        real, imag = det * det - 1.0, 2.0 * det - trace * trace
        size = real * real + imag * imag
        return ((det - q * trace) * imag - real) / size, trace * imag / size

    def gram(ref, upper, cross, lower):
        lane = lax.broadcasted_iota(jnp.int32, (1, 128), 1)
        ref[0:1, :] = jnp.where(lane == 0, upper, cross)[:, 0:2]
        ref[1:2, :] = jnp.where(lane == 0, cross, lower)[:, 0:2]

    a0, f0 = factors(mu[0], m00, w00, e00)
    a1, f1 = factors(mu[1], m11, w11, e11)
    a, f = jnp.where(first, a0, a1), jnp.where(first, f0, f1)
    my_mu = jnp.where(first, mu[0], mu[1])
    column_block = lane_block(pole)
    for block, base, applied in (
        (lane_block(pole), own_b[:, :, column_block], u_ref[:, :, column_block]),
        (lane_block(partner), far_b[:, :, column_block], u_far[...]),
    ):
        out_ref[0, :, :, block] = a * base + f * (applied - my_mu * base)
    cross = a0 * a1 * m01 + a0 * f1 * c01 + f0 * a1 * c10 + f0 * f1 * w01
    gram(corr_ref, a0 * a0 * m00 + f0 * f0 * w00, cross, a1 * a1 * m11 + f1 * f1 * w11)
    cross = (
        a0 * a1 * (c01 + mu[1] * m01)
        + a0 * f1 * (w01 + mu[0] * c01)
        + f0 * a1 * (w01 + mu[1] * c10)
        + f0 * f1 * e01
    )
    gram(
        energy_ref,
        a0 * a0 * mu[0] * m00 + 2.0 * a0 * f0 * w00 + f0 * f0 * e00,
        cross,
        a1 * a1 * mu[1] * m11 + 2.0 * a1 * f1 * w11 + f1 * f1 * e11,
    )
    sent(parts, fy * chips - 1, 9)


def local(states, potential):
    columns, cy, cz, nx = states.shape
    fy, fz, poles = lax.axis_size("fy"), lax.axis_size("fz"), lax.axis_size("pole")
    half = nx // 2
    f32 = jnp.float32
    in_vmem = pl.BlockSpec(memory_space=pltpu.VMEM)
    in_hbm = pl.BlockSpec(memory_space=pl.ANY)

    def vmem(*shape):
        return pltpu.VMEM(shape, f32)

    x_block, y_block = vmem(cy, cz, nx), vmem(fy, cy, nx)
    filtered, corr, energy = pl.pallas_call(
        functools.partial(kernel, cy, cz, nx, fy, fz, poles),
        out_shape=(
            jax.ShapeDtypeStruct((1, cy, cz, nx), f32),
            jax.ShapeDtypeStruct((columns, columns), f32),
            jax.ShapeDtypeStruct((columns, columns), f32),
        ),
        in_specs=[in_hbm] * 5,
        out_specs=(in_vmem,) * 3,
        scratch_shapes=[
            x_block, x_block, vmem(cy, cz, half),
            vmem(nx, nx), vmem(cy * fy, cy * fy), vmem(cz * fz, cz * fz),
            x_block, x_block,
            y_block, y_block, vmem(fz, cz, nx),
            y_block, vmem(fz, cz, nx), y_block, vmem(fz, cz, nx),
            y_block, y_block, vmem(fz, cz, nx),
            vmem(cy // 2, cz, nx), vmem(cy // 2, cz, half), vmem(cy, cz, half), vmem(columns, cy // 2 * cz, nx),
            vmem(16, 128), vmem(1, 128), vmem(1, 128), vmem(1, 128), vmem(fy * poles * fz // 2, 1, 128), vmem(8, 128),
            pltpu.SemaphoreType.DMA((8,)),
            pltpu.SemaphoreType.DMA((10,)),
            pltpu.SemaphoreType.DMA((10,)),
        ],
        compiler_params=pltpu.CompilerParams(
            collective_id=0, has_side_effects=True, vmem_limit_bytes=32 * 1024 * 1024
        ),
    )(
        *(
            pltpu.with_memory_space_constraint(operand, pltpu.HBM)
            for operand in (
                states,
                potential,
                jnp.asarray(axis_operator(nx)),
                jnp.asarray(axis_operator(cy * fy)),
                jnp.asarray(axis_operator(cz * fz)),
            )
        )
    )
    cells = 1.0 / float(nx * cy * fy * cz * fz)
    return filtered, corr * cells, energy * cells


def solution(mesh):
    placed = (P(None, "fy", "fz", None), P("fy", "fz", None))
    return jax.shard_map(
        local,
        mesh=mesh,
        in_specs=placed,
        out_specs=(P("pole", "fy", "fz", None), P(), P()),
        check_vma=False,
    )
```

```python
import functools
import math

import jax
import jax.numpy as jnp
import numpy as np
from jax import lax
from jax.experimental import pallas as pl
from jax.experimental.pallas import tpu as pltpu
from jax.sharding import PartitionSpec as P

MESH = pl.DeviceIdType.MESH
HIGH = lax.Precision.HIGHEST


def axis_operator(length):
    index = np.arange(length)
    signed = np.where(index < length // 2, index, index - length) * (2.0 * math.pi / length)
    phases = (index[:, None] * index[None, :] % length) * (2.0 * math.pi / length)
    first = (np.cos(phases) @ (0.5 * signed * signed)) / length
    return np.asarray(first[(index[:, None] - index[None, :]) % length], np.float32)


def far_first(count):
    return sorted(range(1, count), key=lambda k: -min(k, count - k))


def dot(left, right):
    return jnp.dot(left, right, precision=HIGH, preferred_element_type=jnp.float32)


def lanes(product):
    return jnp.sum(product, axis=0, keepdims=True)


def kernel(
    cy, cz, nx, fy, fz, poles,
    states_hbm, pot_hbm, dx_hbm, dy_hbm, dz_hbm,
    out_ref, corr_ref, energy_ref,
    own_b, far_b, v_ref, dx_ref, dy_ref, dz_ref, s_ref, u_ref,
    ysend, yb, zb, ymul, zmul, yback, zback, yusend, yu, zu, far_u, far_w, u_far, xmul,
    acc, mine_sums, core_sums, chip_sums, parts, rows_ref,
    load_sem, send_sem, recv_sem,
):
    pole, my, mz = lax.axis_index("pole"), lax.axis_index("fy"), lax.axis_index("fz")
    partner = 1 - pole
    plane = pole * fz + mz
    rows = cy * cz
    half = nx // 2
    split = cy // 2
    col0, col1 = slice(0, half), slice(half, nx)

    def lane_block(index):
        return pl.ds(pl.multiple_of(index * half, half), half)

    def at_y(step):
        return (pole, lax.rem(my + step, fy), mz)

    def at_z(step):
        return (pole, my, lax.rem(mz + step, fz))

    def at_plane(step):
        other = lax.rem(plane + step, poles * fz)
        return (other // fz, my, lax.rem(other, fz))

    def push(src, dst, place, slot):
        pltpu.make_async_remote_copy(
            src_ref=src,
            dst_ref=dst,
            send_sem=send_sem.at[slot],
            recv_sem=recv_sem.at[slot],
            device_id=place,
            device_id_type=MESH,
        ).start()

    def push_y(src, dst, step, slot):
        push(src.at[lax.rem(my + step, fy)], dst.at[my], at_y(step), slot)

    def push_z(src, dst, step, slot):
        push(src.at[lax.rem(mz + step, fz)], dst.at[mz], at_z(step), slot)

    def scatter_y(src, dst, slot):
        for step in far_first(fy):
            push_y(src, dst, step, slot)
        dst[my] = src[my]

    def scatter_z(src, dst, slot):
        for step in far_first(fz):
            push_z(src, dst, step, slot)
        dst[mz] = src[mz]

    def arrived(dst, count, slot):
        whole = dst.at[pl.ds(0, count)]
        pltpu.make_async_copy(whole, whole, recv_sem.at[slot]).wait()

    def sent(dst, count, slot):
        whole = dst.at[pl.ds(0, count)]
        pltpu.make_async_copy(whole, whole, send_sem.at[slot]).wait()

    barrier = pltpu.get_barrier_semaphore()

    for step in far_first(fy):
        pl.semaphore_signal(barrier, inc=1, device_id=at_y(step), device_id_type=MESH)
    for step in far_first(fz):
        pl.semaphore_signal(barrier, inc=1, device_id=at_z(step), device_id_type=MESH)
    across = (partner, my, mz)
    pl.semaphore_signal(barrier, inc=1, device_id=across, device_id_type=MESH)

    def load(src, dst, slot):
        copy = pltpu.make_async_copy(src, dst, load_sem.at[slot])
        copy.start()
        return copy

    near = [load(states_hbm.at[c, :, :, lane_block(pole)], own_b.at[:, :, pl.ds(c * half, half)], c) for c in range(2)]
    rest = [
        load(states_hbm.at[c, :, :, lane_block(partner)], far_b.at[:, :, pl.ds(c * half, half)], 2 + c) for c in range(2)
    ]
    rest.append(load(pot_hbm.at[:, :, lane_block(pole)], v_ref, 4))
    rest.append(load(dx_hbm, dx_ref, 5))
    rest.append(load(dz_hbm, dz_ref, 6))
    rest.append(load(dy_hbm, dy_ref, 7))
    for copy in near:
        copy.wait()
    ysend[...] = jnp.swapaxes(own_b[...], 0, 1)
    pl.semaphore_wait(barrier, fy + fz - 1)

    scatter_y(ysend, yb, 0)
    scatter_z(own_b, zb, 1)
    for copy in rest:
        copy.wait()

    def flat(ref):
        return ref[...].reshape(rows, nx)

    def column(ref, c):
        return ref[:, :, c * half : (c + 1) * half].reshape(-1, half)

    v = v_ref[...].reshape(rows, half)
    b = [column(own_b, c) for c in range(2)]
    s = []
    for c in range(2):
        whole = jnp.concatenate([b[c], column(far_b, c)], axis=1)
        s.append(v * b[c] + dot(whole, dx_ref[:, col0]))
        s_ref[:, :, c * half : (c + 1) * half] = s[c].reshape(cy, cz, half)
    acc[0:1] = lanes(b[0] * b[0])
    acc[1:2] = lanes(b[0] * b[1])
    acc[2:3] = lanes(b[1] * b[1])
    acc[12:16] = jnp.zeros((4, 128), jnp.float32)

    arrived(zb, fz - 1, 1)
    zmul[...] = dot(dz_ref[...], flat(zb)).reshape(fz, cz, nx)
    scatter_z(zmul, zback, 3)
    arrived(yb, fy - 1, 0)
    ymul[...] = dot(dy_ref[...], flat(yb)).reshape(fy, cy, nx)
    scatter_y(ymul, yback, 2)

    arrived(zback, fz - 1, 3)
    s_ref[...] += zback[...]
    yusend[...] = jnp.swapaxes(s_ref[...], 0, 1)
    scatter_y(yusend, yu, 4)
    arrived(yback, fy - 1, 2)
    u_ref[...] = s_ref[...] + jnp.swapaxes(yback[...], 0, 1)
    scatter_z(u_ref, zu, 5)
    push(u_ref.at[pl.ds(partner * split, split)], far_u, across, 6)
    push(u_ref.at[pl.ds(pole * split, split), :, lane_block(partner)], far_w, across, 7)

    u = [column(u_ref, c) for c in range(2)]
    acc[3:4] = lanes(b[0] * u[0])
    acc[4:5] = lanes(b[0] * u[1])
    acc[5:6] = lanes(b[1] * u[1])
    acc[6:7] = lanes(u[0] * u[0])
    acc[7:8] = lanes(u[0] * u[1])
    acc[8:9] = lanes(u[1] * u[1])
    applied = [v * u[0], v * u[1]]
    terms = [lanes(u[0] * applied[0]), lanes(u[0] * applied[1]), lanes(u[1] * applied[1])]

    def quadratic(left, right):
        terms[0] += lanes(left[0] * right[0])
        terms[1] += lanes(left[0] * right[1])
        terms[2] += lanes(left[1] * right[1])

    for c in range(2):
        xmul[:, :, c * nx : (c + 1) * nx] = dot(u[c], dx_ref[0:half, :]).reshape(cy, cz, 2 * half)
    quadratic(u, [xmul[:, :, c * nx : c * nx + half].reshape(rows, half) for c in range(2)])
    mine, others = pl.ds(pole * split, split), pl.ds(partner * split, split)
    between = [xmul[mine, :, c * nx + half : (c + 1) * nx].reshape(-1, half) for c in range(2)]

    def pencil(operator, left):
        product = dot(operator[...], left)
        quadratic([left[:, col0], left[:, col1]], [product[:, col0], product[:, col1]])

    arrived(yu, fy - 1, 4)
    pencil(dy_ref, flat(yu) + flat(ymul))
    arrived(far_u, split, 6)
    far = [column(far_u, c) for c in range(2)]
    terms[0] += 2.0 * lanes(far[0] * between[0])
    terms[1] += lanes(far[0] * between[1] + far[1] * between[0])
    terms[2] += 2.0 * lanes(far[1] * between[1])
    arrived(zu, fz - 1, 5)
    pencil(dz_ref, flat(zu))
    for i in range(3):
        acc[9 + i : 10 + i] = terms[i]

    lane = lax.broadcasted_iota(jnp.int32, (16, 128), 1)
    row = lax.broadcasted_iota(jnp.int32, (16, 128), 0)
    folded = acc[...]
    for shift in (64, 32, 16, 8):
        folded = folded + pltpu.roll(folded, shift, 1)
    mine_sums[...] = jnp.sum(jnp.where(lane // 8 == row, folded, 0.0), axis=0, keepdims=True)
    push(mine_sums, core_sums, (pole, my, mz + 1 - 2 * lax.rem(mz, 2)), 8)

    first = pole == 0
    arrived(far_w, split, 7)
    u_far[mine] = far_u[:, :, lane_block(pole)]
    u_far[others] = far_w[...]

    whole_core = core_sums.at[pl.ds(0, 1)]
    pltpu.make_async_copy(whole_core, whole_core, recv_sem.at[8]).wait()
    chips = poles * fz // 2
    chip = my * chips + plane // 2
    chip_sums[...] = mine_sums[...] + core_sums[...]
    for step_y in far_first(fy) + [0]:

        def body(step, carry, step_y=step_y):
            other = lax.rem(plane + 2 * step, 2 * chips)
            place = (other // fz, lax.rem(my + step_y, fy), lax.rem(other, fz))
            push(chip_sums, parts.at[chip], place, 9)
            return carry

        lax.fori_loop(0 if step_y else 1, chips, body, 0)
    parts[chip] = chip_sums[...]

    sent(yb, fy - 1, 0)
    sent(zb, fz - 1, 1)
    sent(yback, fy - 1, 2)
    sent(zback, fz - 1, 3)
    sent(yu, fy - 1, 4)
    sent(zu, fz - 1, 5)
    sent(far_u, split, 6)
    sent(far_w, split, 7)
    pltpu.make_async_copy(whole_core, whole_core, send_sem.at[8]).wait()

    arrived(parts, fy * chips - 1, 9)
    total = jnp.sum(parts[...], axis=0)
    slim = lax.broadcasted_iota(jnp.int32, (8, 128), 1) < 8

    def totals(values):
        for i, value in enumerate(values):
            rows_ref[i : i + 1] = value
        summed = jnp.sum(jnp.where(slim, rows_ref[...], 0.0), axis=1, keepdims=True)
        rows_ref[...] = jnp.broadcast_to(summed, (8, 128))
        return [rows_ref[i : i + 1] for i in range(len(values))]

    l00, l01, l11, b00, b01, b11, u00, u01, u11, e00, e01, e11 = (
        pltpu.roll(total, (128 - 8 * i) % 128, 1) if i else total for i in range(12)
    )
    m00, m01, m11, h00, h11 = totals([l00, l01, l11, b00, b11])
    mu = [h00 / m00, h11 / m11]
    w00, w01, w11, e00, e01, e11, c01, c10 = totals(
        [
            u00 - mu[0] * (2.0 * b00 - mu[0] * l00),
            u01 - (mu[0] + mu[1]) * b01 + mu[0] * mu[1] * l01,
            u11 - mu[1] * (2.0 * b11 - mu[1] * l11),
            e00 - mu[0] * (2.0 * u00 - mu[0] * b00),
            e01 - (mu[0] + mu[1]) * u01 + mu[0] * mu[1] * b01,
            e11 - mu[1] * (2.0 * u11 - mu[1] * b11),
            b01 - mu[1] * l01,
            b01 - mu[0] * l01,
        ]
    )

    top = 1.5 * math.pi**2 + 3.0

    def factors(mean, norm, ww, whw):
        nu = jnp.where(ww > 0.0, jnp.clip(whw / jnp.where(ww > 0.0, ww, 1.0), 0.0, top), mean)
        t2 = jnp.maximum(ww, 0.0) / norm
        p, q = mean - 1.0, nu - 1.0
        trace, det = p + q, p * q - t2
        real, imag = det * det - 1.0, 2.0 * det - trace * trace
        size = real * real + imag * imag
        return ((det - q * trace) * imag - real) / size, trace * imag / size

    def gram(ref, upper, cross, lower):
        lane = lax.broadcasted_iota(jnp.int32, (1, 128), 1)
        ref[0:1, :] = jnp.where(lane == 0, upper, cross)[:, 0:2]
        ref[1:2, :] = jnp.where(lane == 0, cross, lower)[:, 0:2]

    a0, f0 = factors(mu[0], m00, w00, e00)
    a1, f1 = factors(mu[1], m11, w11, e11)
    a, f = jnp.where(first, a0, a1), jnp.where(first, f0, f1)
    my_mu = jnp.where(first, mu[0], mu[1])
    column_block = lane_block(pole)
    for block, base, applied in (
        (lane_block(pole), own_b[:, :, column_block], u_ref[:, :, column_block]),
        (lane_block(partner), far_b[:, :, column_block], u_far[...]),
    ):
        out_ref[0, :, :, block] = a * base + f * (applied - my_mu * base)
    cross = a0 * a1 * m01 + a0 * f1 * c01 + f0 * a1 * c10 + f0 * f1 * w01
    gram(corr_ref, a0 * a0 * m00 + f0 * f0 * w00, cross, a1 * a1 * m11 + f1 * f1 * w11)
    cross = (
        a0 * a1 * (c01 + mu[1] * m01)
        + a0 * f1 * (w01 + mu[0] * c01)
        + f0 * a1 * (w01 + mu[1] * c10)
        + f0 * f1 * e01
    )
    gram(
        energy_ref,
        a0 * a0 * mu[0] * m00 + 2.0 * a0 * f0 * w00 + f0 * f0 * e00,
        cross,
        a1 * a1 * mu[1] * m11 + 2.0 * a1 * f1 * w11 + f1 * f1 * e11,
    )
    sent(parts, fy * chips - 1, 9)


def local(states, potential):
    columns, cy, cz, nx = states.shape
    fy, fz, poles = lax.axis_size("fy"), lax.axis_size("fz"), lax.axis_size("pole")
    half = nx // 2
    f32 = jnp.float32
    in_vmem = pl.BlockSpec(memory_space=pltpu.VMEM)
    in_hbm = pl.BlockSpec(memory_space=pl.ANY)

    def vmem(*shape):
        return pltpu.VMEM(shape, f32)

    x_block, y_block = vmem(cy, cz, nx), vmem(fy, cy, nx)
    filtered, corr, energy = pl.pallas_call(
        functools.partial(kernel, cy, cz, nx, fy, fz, poles),
        out_shape=(
            jax.ShapeDtypeStruct((1, cy, cz, nx), f32),
            jax.ShapeDtypeStruct((columns, columns), f32),
            jax.ShapeDtypeStruct((columns, columns), f32),
        ),
        in_specs=[in_hbm] * 5,
        out_specs=(in_vmem,) * 3,
        scratch_shapes=[
            x_block, x_block, vmem(cy, cz, half),
            vmem(nx, nx), vmem(cy * fy, cy * fy), vmem(cz * fz, cz * fz),
            x_block, x_block,
            y_block, y_block, vmem(fz, cz, nx),
            y_block, vmem(fz, cz, nx), y_block, vmem(fz, cz, nx),
            y_block, y_block, vmem(fz, cz, nx),
            vmem(cy // 2, cz, nx), vmem(cy // 2, cz, half), vmem(cy, cz, half), vmem(cy, cz, columns * nx),
            vmem(16, 128), vmem(1, 128), vmem(1, 128), vmem(1, 128), vmem(fy * poles * fz // 2, 1, 128), vmem(8, 128),
            pltpu.SemaphoreType.DMA((8,)),
            pltpu.SemaphoreType.DMA((10,)),
            pltpu.SemaphoreType.DMA((10,)),
        ],
        compiler_params=pltpu.CompilerParams(
            collective_id=0, has_side_effects=True, vmem_limit_bytes=32 * 1024 * 1024
        ),
    )(
        *(
            pltpu.with_memory_space_constraint(operand, pltpu.HBM)
            for operand in (
                states,
                potential,
                jnp.asarray(axis_operator(nx)),
                jnp.asarray(axis_operator(cy * fy)),
                jnp.asarray(axis_operator(cz * fz)),
            )
        )
    )
    cells = 1.0 / float(nx * cy * fy * cz * fz)
    return filtered, corr * cells, energy * cells


def solution(mesh):
    placed = (P(None, "fy", "fz", None), P("fy", "fz", None))
    return jax.shard_map(
        local,
        mesh=mesh,
        in_specs=placed,
        out_specs=(P("pole", "fy", "fz", None), P(), P()),
        check_vma=False,
    )
```

```python
import functools
import math

import jax
import jax.numpy as jnp
import numpy as np
from jax import lax
from jax.experimental import pallas as pl
from jax.experimental.pallas import tpu as pltpu
from jax.sharding import PartitionSpec as P

MESH = pl.DeviceIdType.MESH
HIGH = lax.Precision.HIGHEST


def axis_operator(length):
    index = np.arange(length)
    signed = np.where(index < length // 2, index, index - length) * (2.0 * math.pi / length)
    phases = (index[:, None] * index[None, :] % length) * (2.0 * math.pi / length)
    first = (np.cos(phases) @ (0.5 * signed * signed)) / length
    return np.asarray(first[(index[:, None] - index[None, :]) % length], np.float32)


def far_first(count):
    return sorted(range(1, count), key=lambda k: -min(k, count - k))


def dot(left, right):
    return jnp.dot(left, right, precision=HIGH, preferred_element_type=jnp.float32)


def lanes(product):
    return jnp.sum(product, axis=0, keepdims=True)


def kernel(
    cy, cz, nx, fy, fz, poles,
    states_hbm, pot_hbm, dx_hbm, dy_hbm, dz_hbm,
    out_ref, corr_ref, energy_ref,
    own_b, far_b, v_ref, dx_ref, dy_ref, dz_ref, g_ref, s_ref, q_ref, u_ref, y_ref, dxs_ref, dxg_ref, far_u,
    ysend, ysend2, yb, yq, ymul, ymul2, yback, yback2, z_order,
    zb, zq, zmul, zmul2, zback, zback2,
    acc, mine_sums, core_sums, chip_sums, parts, rows_ref,
    load_sem, send_sem, recv_sem,
):
    pole, my, mz = lax.axis_index("pole"), lax.axis_index("fy"), lax.axis_index("fz")
    partner = 1 - pole
    plane = pole * fz + mz
    rows = cy * cz
    half = nx // 2
    col0, col1 = slice(0, half), slice(half, nx)

    def lane_block(index):
        return pl.ds(pl.multiple_of(index * half, half), half)

    def at_y(step):
        return (pole, lax.rem(my + step, fy), mz)

    def at_z(step):
        return (pole, my, lax.rem(mz + step, fz))

    def push(src, dst, place, slot):
        pltpu.make_async_remote_copy(
            src_ref=src,
            dst_ref=dst,
            send_sem=send_sem.at[slot],
            recv_sem=recv_sem.at[slot],
            device_id=place,
            device_id_type=MESH,
        ).start()

    def push_y(src, dst, step, slot):
        push(src.at[lax.rem(my + step, fy)], dst.at[my], at_y(step), slot)

    def push_z(src, dst, step, slot):
        push(src.at[lax.rem(mz + step, fz)], dst.at[mz], at_z(step), slot)

    def scatter_y(src, dst, slot):
        for step in far_first(fy):
            push_y(src, dst, step, slot)
        dst[my] = src[my]

    def scatter_z(src, dst, slot):
        for step in far_first(fz):
            push_z(src, dst, step, slot)
        dst[mz] = src[mz]

    def arrived(dst, count, slot):
        whole = dst.at[pl.ds(0, count)]
        pltpu.make_async_copy(whole, whole, recv_sem.at[slot]).wait()

    def sent(dst, count, slot):
        whole = dst.at[pl.ds(0, count)]
        pltpu.make_async_copy(whole, whole, send_sem.at[slot]).wait()

    barrier = pltpu.get_barrier_semaphore()

    for step in far_first(fy):
        pl.semaphore_signal(barrier, inc=1, device_id=at_y(step), device_id_type=MESH)
    for step in far_first(fz):
        pl.semaphore_signal(barrier, inc=1, device_id=at_z(step), device_id_type=MESH)
    across = (partner, my, mz)
    pl.semaphore_signal(barrier, inc=1, device_id=across, device_id_type=MESH)

    def load(src, dst, slot):
        copy = pltpu.make_async_copy(src, dst, load_sem.at[slot])
        copy.start()
        return copy

    near = [load(states_hbm.at[c, :, :, lane_block(pole)], own_b.at[:, :, pl.ds(c * half, half)], c) for c in range(2)]
    rest = [
        load(states_hbm.at[c, :, :, lane_block(partner)], far_b.at[:, :, pl.ds(c * half, half)], 2 + c) for c in range(2)
    ]
    rest.append(load(pot_hbm.at[:, :, lane_block(pole)], v_ref.at[:, :, pl.ds(0, half)], 4))
    rest.append(load(pot_hbm.at[:, :, lane_block(partner)], v_ref.at[:, :, pl.ds(half, half)], 5))
    rest.append(load(dx_hbm, dx_ref, 6))
    rest.append(load(dz_hbm, dz_ref, 7))
    rest.append(load(dy_hbm, dy_ref, 8))
    for copy in near:
        copy.wait()
    ysend[...] = jnp.swapaxes(own_b[...], 0, 1)
    for copy in rest:
        copy.wait()

    def flat(ref):
        return ref[...].reshape(rows, nx)

    def column(ref, c):
        return ref[:, :, c * half : (c + 1) * half].reshape(-1, half)

    terms = [jnp.zeros((1, half), jnp.float32)] * 3

    def quadratic(left, right):
        terms[0] += lanes(left[0] * right[0])
        terms[1] += lanes(left[0] * right[1])
        terms[2] += lanes(left[1] * right[1])

    def symmetric(left, right):
        terms[0] += 2.0 * lanes(left[0] * right[0])
        terms[1] += lanes(left[0] * right[1] + left[1] * right[0])
        terms[2] += 2.0 * lanes(left[1] * right[1])

    v = v_ref[...].reshape(rows, nx)
    b = [column(own_b, c) for c in range(2)]
    g, s = [], []
    for c in range(2):
        whole = jnp.concatenate([b[c], column(far_b, c)], axis=1)
        g.append(dot(whole, dx_ref[...]))
        s.append(v * whole + g[c])
        here = slice(c * half, (c + 1) * half)
        s_ref[:, :, here] = s[c][:, col0].reshape(cy, cz, half)
        g_ref[:, :, here] = g[c][:, col0].reshape(cy, cz, half)
        q_ref[:, :, here] = (s[c][:, col0] + 0.5 * g[c][:, col0]).reshape(cy, cz, half)
    ysend2[...] = jnp.swapaxes(q_ref[...], 0, 1)

    pl.semaphore_wait(barrier, fy + fz - 1)
    scatter_y(ysend, yb, 0)
    scatter_z(own_b, zb, 1)
    scatter_z(q_ref, zq, 3)
    scatter_y(ysend2, yq, 2)

    acc[0:1] = lanes(b[0] * b[0])
    acc[1:2] = lanes(b[0] * b[1])
    acc[2:3] = lanes(b[1] * b[1])
    acc[12:16] = jnp.zeros((4, 128), jnp.float32)
    for c in range(2):
        here = slice(c * half, (c + 1) * half)
        dxs_ref[:, :, here] = dot(s[c], dx_ref[:, col0]).reshape(cy, cz, half)
        dxg_ref[:, :, here] = dot(g[c], dx_ref[:, col0]).reshape(cy, cz, half)
    quadratic([s[c][:, col0] for c in range(2)], [column(dxs_ref, c) for c in range(2)])

    arrived(zb, fz - 1, 1)
    zmul[...] = dot(dz_ref[...], flat(zb)).reshape(fz, cz, nx)
    scatter_z(zmul, zback, 5)
    arrived(yb, fy - 1, 0)
    ymul[...] = dot(dy_ref[...], flat(yb)).reshape(fy, cy, nx)
    scatter_y(ymul, yback, 4)
    ymul2[...] = dot(dy_ref[...], flat(ymul)).reshape(fy, cy, nx)
    scatter_y(ymul2, yback2, 6)
    z_twice = dot(dz_ref[...], flat(zmul))
    arrived(zq, fz - 1, 3)
    p = flat(zq) + flat(zmul)
    p_mul = dot(dz_ref[...], p)
    zmul2[...] = (4.0 * p_mul - z_twice).reshape(fz, cz, nx)
    scatter_z(zmul2, zback2, 7)
    quadratic([p[:, col0], p[:, col1]], [p_mul[:, col0], p_mul[:, col1]])
    arrived(yq, fy - 1, 2)
    p = flat(yq) + flat(ymul)
    p_mul = dot(dy_ref[...], flat(yq)) + flat(ymul2)
    quadratic([p[:, col0], p[:, col1]], [p_mul[:, col0], p_mul[:, col1]])

    arrived(zback, fz - 1, 5)
    arrived(yback, fy - 1, 4)
    y_ref[...] = jnp.swapaxes(yback[...], 0, 1)
    u_ref[...] = s_ref[...] + zback[...] + y_ref[...]
    push(u_ref.at[:, :, lane_block(partner)], far_u, across, 10)
    u = [column(u_ref, c) for c in range(2)]
    acc[3:4] = lanes(b[0] * u[0])
    acc[4:5] = lanes(b[0] * u[1])
    acc[5:6] = lanes(b[1] * u[1])
    acc[6:7] = lanes(u[0] * u[0])
    acc[7:8] = lanes(u[0] * u[1])
    acc[8:9] = lanes(u[1] * u[1])
    quadratic(u, [v[:, col0] * u[c] for c in range(2)])
    symmetric(
        [0.5 * column(dxs_ref, c) - 0.125 * column(dxg_ref, c) for c in range(2)],
        [column(y_ref, c) + column(zback, c) for c in range(2)],
    )
    z_order[...] = 1.5 * jnp.swapaxes(zback[...], 0, 1)
    arrived(zback2, fz - 1, 7)
    symmetric([0.5 * column(y_ref, c) for c in range(2)], [column(zback2, c) for c in range(2)])
    arrived(yback2, fy - 1, 6)
    symmetric([column(z_order, c) for c in range(2)], [column(yback2, c) for c in range(2)])
    for i in range(3):
        acc[9 + i : 10 + i] = terms[i]

    lane = lax.broadcasted_iota(jnp.int32, (16, 128), 1)
    row = lax.broadcasted_iota(jnp.int32, (16, 128), 0)
    folded = acc[...]
    for shift in (64, 32, 16, 8):
        folded = folded + pltpu.roll(folded, shift, 1)
    mine_sums[...] = jnp.sum(jnp.where(lane // 8 == row, folded, 0.0), axis=0, keepdims=True)
    push(mine_sums, core_sums, (pole, my, mz + 1 - 2 * lax.rem(mz, 2)), 8)

    first = pole == 0
    whole_core = core_sums.at[pl.ds(0, 1)]
    pltpu.make_async_copy(whole_core, whole_core, recv_sem.at[8]).wait()
    chips = poles * fz // 2
    chip = my * chips + plane // 2
    chip_sums[...] = mine_sums[...] + core_sums[...]
    for step_y in far_first(fy) + [0]:

        def body(step, carry, step_y=step_y):
            other = lax.rem(plane + 2 * step, 2 * chips)
            place = (other // fz, lax.rem(my + step_y, fy), lax.rem(other, fz))
            push(chip_sums, parts.at[chip], place, 9)
            return carry

        lax.fori_loop(0 if step_y else 1, chips, body, 0)
    parts[chip] = chip_sums[...]

    for slot, (y_buffer, z_buffer) in zip((0, 2, 4, 6), ((yb, zb), (yq, zq), (yback, zback), (yback2, zback2))):
        sent(y_buffer, fy - 1, slot)
        sent(z_buffer, fz - 1, slot + 1)
    arrived(far_u, cy, 10)
    sent(far_u, cy, 10)
    pltpu.make_async_copy(whole_core, whole_core, send_sem.at[8]).wait()

    arrived(parts, fy * chips - 1, 9)
    total = jnp.sum(parts[...], axis=0)
    slim = lax.broadcasted_iota(jnp.int32, (8, 128), 1) < 8

    def totals(values):
        for i, value in enumerate(values):
            rows_ref[i : i + 1] = value
        summed = jnp.sum(jnp.where(slim, rows_ref[...], 0.0), axis=1, keepdims=True)
        rows_ref[...] = jnp.broadcast_to(summed, (8, 128))
        return [rows_ref[i : i + 1] for i in range(len(values))]

    l00, l01, l11, b00, b01, b11, u00, u01, u11, e00, e01, e11 = (
        pltpu.roll(total, (128 - 8 * i) % 128, 1) if i else total for i in range(12)
    )
    m00, m01, m11, h00, h11 = totals([l00, l01, l11, b00, b11])
    mu = [h00 / m00, h11 / m11]
    w00, w01, w11, e00, e01, e11, c01, c10 = totals(
        [
            u00 - mu[0] * (2.0 * b00 - mu[0] * l00),
            u01 - (mu[0] + mu[1]) * b01 + mu[0] * mu[1] * l01,
            u11 - mu[1] * (2.0 * b11 - mu[1] * l11),
            e00 - mu[0] * (2.0 * u00 - mu[0] * b00),
            e01 - (mu[0] + mu[1]) * u01 + mu[0] * mu[1] * b01,
            e11 - mu[1] * (2.0 * u11 - mu[1] * b11),
            b01 - mu[1] * l01,
            b01 - mu[0] * l01,
        ]
    )

    top = 1.5 * math.pi**2 + 3.0

    def factors(mean, norm, ww, whw):
        nu = jnp.where(ww > 0.0, jnp.clip(whw / jnp.where(ww > 0.0, ww, 1.0), 0.0, top), mean)
        t2 = jnp.maximum(ww, 0.0) / norm
        p, q = mean - 1.0, nu - 1.0
        trace, det = p + q, p * q - t2
        real, imag = det * det - 1.0, 2.0 * det - trace * trace
        size = real * real + imag * imag
        return ((det - q * trace) * imag - real) / size, trace * imag / size

    def gram(ref, upper, cross, lower):
        lane = lax.broadcasted_iota(jnp.int32, (1, 128), 1)
        ref[0:1, :] = jnp.where(lane == 0, upper, cross)[:, 0:2]
        ref[1:2, :] = jnp.where(lane == 0, cross, lower)[:, 0:2]

    a0, f0 = factors(mu[0], m00, w00, e00)
    a1, f1 = factors(mu[1], m11, w11, e11)
    a, f = jnp.where(first, a0, a1), jnp.where(first, f0, f1)
    my_mu = jnp.where(first, mu[0], mu[1])
    column_block = lane_block(pole)
    for block, base, applied in (
        (lane_block(pole), own_b[:, :, column_block], u_ref[:, :, column_block]),
        (lane_block(partner), far_b[:, :, column_block], far_u[...]),
    ):
        out_ref[0, :, :, block] = a * base + f * (applied - my_mu * base)
    cross = a0 * a1 * m01 + a0 * f1 * c01 + f0 * a1 * c10 + f0 * f1 * w01
    gram(corr_ref, a0 * a0 * m00 + f0 * f0 * w00, cross, a1 * a1 * m11 + f1 * f1 * w11)
    cross = (
        a0 * a1 * (c01 + mu[1] * m01)
        + a0 * f1 * (w01 + mu[0] * c01)
        + f0 * a1 * (w01 + mu[1] * c10)
        + f0 * f1 * e01
    )
    gram(
        energy_ref,
        a0 * a0 * mu[0] * m00 + 2.0 * a0 * f0 * w00 + f0 * f0 * e00,
        cross,
        a1 * a1 * mu[1] * m11 + 2.0 * a1 * f1 * w11 + f1 * f1 * e11,
    )
    sent(parts, fy * chips - 1, 9)


def local(states, potential):
    columns, cy, cz, nx = states.shape
    fy, fz, poles = lax.axis_size("fy"), lax.axis_size("fz"), lax.axis_size("pole")
    half = nx // 2
    f32 = jnp.float32
    in_vmem = pl.BlockSpec(memory_space=pltpu.VMEM)
    in_hbm = pl.BlockSpec(memory_space=pl.ANY)

    def vmem(*shape):
        return pltpu.VMEM(shape, f32)

    x_block, y_block, z_block = vmem(cy, cz, nx), vmem(fy, cy, nx), vmem(fz, cz, nx)
    filtered, corr, energy = pl.pallas_call(
        functools.partial(kernel, cy, cz, nx, fy, fz, poles),
        out_shape=(
            jax.ShapeDtypeStruct((1, cy, cz, nx), f32),
            jax.ShapeDtypeStruct((columns, columns), f32),
            jax.ShapeDtypeStruct((columns, columns), f32),
        ),
        in_specs=[in_hbm] * 5,
        out_specs=(in_vmem,) * 3,
        scratch_shapes=[
            *[x_block] * 3,
            vmem(nx, nx), vmem(cy * fy, cy * fy), vmem(cz * fz, cz * fz),
            *[x_block] * 7, vmem(cy, cz, half),
            *[y_block] * 9,
            *[z_block] * 6,
            vmem(16, 128), vmem(1, 128), vmem(1, 128), vmem(1, 128), vmem(fy * poles * fz // 2, 1, 128), vmem(8, 128),
            pltpu.SemaphoreType.DMA((9,)),
            pltpu.SemaphoreType.DMA((11,)),
            pltpu.SemaphoreType.DMA((11,)),
        ],
        compiler_params=pltpu.CompilerParams(
            collective_id=0, has_side_effects=True, vmem_limit_bytes=32 * 1024 * 1024
        ),
    )(
        *(
            pltpu.with_memory_space_constraint(operand, pltpu.HBM)
            for operand in (
                states,
                potential,
                jnp.asarray(axis_operator(nx)),
                jnp.asarray(axis_operator(cy * fy)),
                jnp.asarray(axis_operator(cz * fz)),
            )
        )
    )
    cells = 1.0 / float(nx * cy * fy * cz * fz)
    return filtered, corr * cells, energy * cells


def solution(mesh):
    placed = (P(None, "fy", "fz", None), P("fy", "fz", None))
    return jax.shard_map(
        local,
        mesh=mesh,
        in_specs=placed,
        out_specs=(P("pole", "fy", "fz", None), P(), P()),
        check_vma=False,
    )
```

```python
import functools
import math

import jax
import jax.numpy as jnp
import numpy as np
from jax import lax
from jax.experimental import pallas as pl
from jax.experimental.pallas import tpu as pltpu
from jax.sharding import PartitionSpec as P

MESH = pl.DeviceIdType.MESH
HIGH = lax.Precision.HIGHEST


def axis_operator(length):
    index = np.arange(length)
    signed = np.where(index < length // 2, index, index - length) * (2.0 * math.pi / length)
    phases = (index[:, None] * index[None, :] % length) * (2.0 * math.pi / length)
    first = (np.cos(phases) @ (0.5 * signed * signed)) / length
    return np.asarray(first[(index[:, None] - index[None, :]) % length], np.float32)


def far_first(count):
    return sorted(range(1, count), key=lambda k: -min(k, count - k))


def dot(left, right):
    return jnp.dot(left, right, precision=HIGH, preferred_element_type=jnp.float32)


def lanes(product):
    return jnp.sum(product, axis=0, keepdims=True)


def kernel(
    cy, cz, nx, fy, fz, poles,
    states_hbm, pot_hbm, dx_hbm, dy_hbm, dz_hbm,
    out_ref, corr_ref, energy_ref,
    own_b, far_b, v_ref, dx_ref, dy_ref, dz_ref, g_ref, s_ref, q_ref, u_ref, y_ref, dxs_ref, dxg_ref, far_u,
    ysend, ysend2, yb, yq, ymul, ymul2, yback, yback2, z_order,
    zb, zq, zmul, zmul2, zback, zback2,
    acc, mine_sums, core_sums, chip_sums, parts, rows_ref,
    load_sem, send_sem, recv_sem,
):
    pole, my, mz = lax.axis_index("pole"), lax.axis_index("fy"), lax.axis_index("fz")
    partner = 1 - pole
    rows = cy * cz
    half = nx // 2
    col0, col1 = slice(0, half), slice(half, nx)

    def lane_block(index):
        return pl.ds(pl.multiple_of(index * half, half), half)

    def at_y(step):
        return (pole, lax.rem(my + step, fy), mz)

    def at_z(step):
        return (pole, my, lax.rem(mz + step, fz))

    def push(src, dst, place, slot):
        pltpu.make_async_remote_copy(
            src_ref=src,
            dst_ref=dst,
            send_sem=send_sem.at[slot],
            recv_sem=recv_sem.at[slot],
            device_id=place,
            device_id_type=MESH,
        ).start()

    def push_y(src, dst, step, slot):
        push(src.at[lax.rem(my + step, fy)], dst.at[my], at_y(step), slot)

    def push_z(src, dst, step, slot):
        push(src.at[lax.rem(mz + step, fz)], dst.at[mz], at_z(step), slot)

    def scatter_y(src, dst, slot):
        for step in far_first(fy):
            push_y(src, dst, step, slot)
        dst[my] = src[my]

    def scatter_z(src, dst, slot):
        for step in far_first(fz):
            push_z(src, dst, step, slot)
        dst[mz] = src[mz]

    def arrived(dst, count, slot):
        whole = dst.at[pl.ds(0, count)]
        pltpu.make_async_copy(whole, whole, recv_sem.at[slot]).wait()

    def sent(dst, count, slot):
        whole = dst.at[pl.ds(0, count)]
        pltpu.make_async_copy(whole, whole, send_sem.at[slot]).wait()

    parts[...] = jnp.zeros(parts.shape, jnp.float32)
    barrier = pltpu.get_barrier_semaphore()

    for step in far_first(fy):
        pl.semaphore_signal(barrier, inc=1, device_id=at_y(step), device_id_type=MESH)
    for step in far_first(fz):
        pl.semaphore_signal(barrier, inc=1, device_id=at_z(step), device_id_type=MESH)
    across = (partner, my, mz)
    pl.semaphore_signal(barrier, inc=1, device_id=across, device_id_type=MESH)

    def load(src, dst, slot):
        copy = pltpu.make_async_copy(src, dst, load_sem.at[slot])
        copy.start()
        return copy

    near = [load(states_hbm.at[c, :, :, lane_block(pole)], own_b.at[:, :, pl.ds(c * half, half)], c) for c in range(2)]
    rest = [
        load(states_hbm.at[c, :, :, lane_block(partner)], far_b.at[:, :, pl.ds(c * half, half)], 2 + c) for c in range(2)
    ]
    rest.append(load(pot_hbm.at[:, :, lane_block(pole)], v_ref.at[:, :, pl.ds(0, half)], 4))
    rest.append(load(pot_hbm.at[:, :, lane_block(partner)], v_ref.at[:, :, pl.ds(half, half)], 5))
    rest.append(load(dx_hbm, dx_ref, 6))
    rest.append(load(dz_hbm, dz_ref, 7))
    rest.append(load(dy_hbm, dy_ref, 8))
    for copy in near:
        copy.wait()
    ysend[...] = jnp.swapaxes(own_b[...], 0, 1)
    for copy in rest:
        copy.wait()

    def flat(ref):
        return ref[...].reshape(rows, nx)

    def column(ref, c):
        return ref[:, :, c * half : (c + 1) * half].reshape(-1, half)

    terms = [jnp.zeros((1, half), jnp.float32)] * 3

    def quadratic(left, right):
        terms[0] += lanes(left[0] * right[0])
        terms[1] += lanes(left[0] * right[1])
        terms[2] += lanes(left[1] * right[1])

    def symmetric(left, right):
        terms[0] += 2.0 * lanes(left[0] * right[0])
        terms[1] += lanes(left[0] * right[1] + left[1] * right[0])
        terms[2] += 2.0 * lanes(left[1] * right[1])

    v = v_ref[...].reshape(rows, nx)
    b = [column(own_b, c) for c in range(2)]
    g, s = [], []
    for c in range(2):
        whole = jnp.concatenate([b[c], column(far_b, c)], axis=1)
        g.append(dot(whole, dx_ref[...]))
        s.append(v * whole + g[c])
        here = slice(c * half, (c + 1) * half)
        s_ref[:, :, here] = s[c][:, col0].reshape(cy, cz, half)
        g_ref[:, :, here] = g[c][:, col0].reshape(cy, cz, half)
        q_ref[:, :, here] = (s[c][:, col0] + 0.5 * g[c][:, col0]).reshape(cy, cz, half)
    ysend2[...] = jnp.swapaxes(q_ref[...], 0, 1)

    pl.semaphore_wait(barrier, fy + fz - 1)
    scatter_y(ysend, yb, 0)
    scatter_z(own_b, zb, 1)
    scatter_z(q_ref, zq, 3)
    scatter_y(ysend2, yq, 2)

    acc[0:1] = lanes(b[0] * b[0])
    acc[1:2] = lanes(b[0] * b[1])
    acc[2:3] = lanes(b[1] * b[1])
    acc[12:16] = jnp.zeros((4, 128), jnp.float32)
    for c in range(2):
        here = slice(c * half, (c + 1) * half)
        dxs_ref[:, :, here] = dot(s[c], dx_ref[:, col0]).reshape(cy, cz, half)
        dxg_ref[:, :, here] = dot(g[c], dx_ref[:, col0]).reshape(cy, cz, half)
    quadratic([s[c][:, col0] for c in range(2)], [column(dxs_ref, c) for c in range(2)])

    arrived(zb, fz - 1, 1)
    zmul[...] = dot(dz_ref[...], flat(zb)).reshape(fz, cz, nx)
    scatter_z(zmul, zback, 5)
    arrived(yb, fy - 1, 0)
    ymul[...] = dot(dy_ref[...], flat(yb)).reshape(fy, cy, nx)
    scatter_y(ymul, yback, 4)
    ymul2[...] = dot(dy_ref[...], flat(ymul)).reshape(fy, cy, nx)
    scatter_y(ymul2, yback2, 6)
    z_twice = dot(dz_ref[...], flat(zmul))
    arrived(zq, fz - 1, 3)
    p = flat(zq) + flat(zmul)
    p_mul = dot(dz_ref[...], p)
    zmul2[...] = (4.0 * p_mul - z_twice).reshape(fz, cz, nx)
    scatter_z(zmul2, zback2, 7)
    quadratic([p[:, col0], p[:, col1]], [p_mul[:, col0], p_mul[:, col1]])
    arrived(yq, fy - 1, 2)
    p = flat(yq) + flat(ymul)
    p_mul = dot(dy_ref[...], flat(yq)) + flat(ymul2)
    quadratic([p[:, col0], p[:, col1]], [p_mul[:, col0], p_mul[:, col1]])

    arrived(zback, fz - 1, 5)
    arrived(yback, fy - 1, 4)
    y_ref[...] = jnp.swapaxes(yback[...], 0, 1)
    u_ref[...] = s_ref[...] + zback[...] + y_ref[...]
    push(u_ref.at[:, :, lane_block(partner)], far_u, across, 10)
    u = [column(u_ref, c) for c in range(2)]
    acc[3:4] = lanes(b[0] * u[0])
    acc[4:5] = lanes(b[0] * u[1])
    acc[5:6] = lanes(b[1] * u[1])
    acc[6:7] = lanes(u[0] * u[0])
    acc[7:8] = lanes(u[0] * u[1])
    acc[8:9] = lanes(u[1] * u[1])
    quadratic(u, [v[:, col0] * u[c] for c in range(2)])
    symmetric(
        [0.5 * column(dxs_ref, c) - 0.125 * column(dxg_ref, c) for c in range(2)],
        [column(y_ref, c) + column(zback, c) for c in range(2)],
    )
    z_order[...] = 1.5 * jnp.swapaxes(zback[...], 0, 1)
    arrived(zback2, fz - 1, 7)
    symmetric([0.5 * column(y_ref, c) for c in range(2)], [column(zback2, c) for c in range(2)])
    arrived(yback2, fy - 1, 6)
    symmetric([column(z_order, c) for c in range(2)], [column(yback2, c) for c in range(2)])
    for i in range(3):
        acc[9 + i : 10 + i] = terms[i]

    lane = lax.broadcasted_iota(jnp.int32, (16, 128), 1)
    row = lax.broadcasted_iota(jnp.int32, (16, 128), 0)
    folded = acc[...]
    for shift in (64, 32, 16, 8):
        folded = folded + pltpu.roll(folded, shift, 1)
    mine_sums[...] = jnp.sum(jnp.where(lane // 8 == row, folded, 0.0), axis=0, keepdims=True)

    core = lax.rem(mz, 2)
    push(mine_sums, core_sums, (pole, my, mz + 1 - 2 * core), 8)
    size_x, size_y = 2 * poles, fz // 4
    place_x = [lax.rem(2 * pole + lax.rem(mz // 2, 2) + k, size_x) for k in range(size_x)]
    place_y = [lax.rem(mz // 4 + k, size_y) for k in range(size_y)]
    place_z = [lax.rem(my + k, fy) for k in range(fy)]
    pole_of = [x // 2 for x in place_x]
    low_of = [2 * lax.rem(x, 2) for x in place_x]
    chip = (my * size_y + mz // 4) * size_x + place_x[0]

    def hops(offset):
        return sum(min(k, n - k) for k, n in zip(offset, (size_x, size_y, fy)))

    offsets = sorted(
        ((x, y, z) for x in range(size_x) for y in range(size_y) for z in range(fy) if (x, y, z) != (0, 0, 0)),
        key=lambda offset: -hops(offset),
    )
    far_away = [offset for offset in offsets if hops(offset) >= hops(offsets[0]) - 2]

    def device(offset, which):
        x, y, z = offset
        return (pole_of[x], place_z[z], place_y[y] * 4 + low_of[x] + which)

    chips = size_x * size_y * fy
    mine_row = pl.ds(core * chips + chip, 1)
    pair_row = pl.ds(chip, 1)
    for offset in far_away:
        for which in range(2):
            push(mine_sums, parts.at[mine_row], device(offset, which), 9)

    whole_core = core_sums.at[pl.ds(0, 1)]
    pltpu.make_async_copy(whole_core, whole_core, recv_sem.at[8]).wait()
    chip_sums[...] = mine_sums[...] + core_sums[...]
    for offset in offsets[len(far_away) :]:
        push(chip_sums, parts.at[pair_row], device(offset, core), 9)
    parts[pair_row, :] = chip_sums[...]
    messages = len(offsets) + len(far_away)

    for slot, (y_buffer, z_buffer) in zip((0, 2, 4, 6), ((yb, zb), (yq, zq), (yback, zback), (yback2, zback2))):
        sent(y_buffer, fy - 1, slot)
        sent(z_buffer, fz - 1, slot + 1)
    arrived(far_u, cy, 10)
    sent(far_u, cy, 10)
    pltpu.make_async_copy(whole_core, whole_core, send_sem.at[8]).wait()

    arrived(parts, messages, 9)
    total = jnp.sum(parts[0:chips] + parts[chips : 2 * chips], axis=0, keepdims=True)
    slim = lax.broadcasted_iota(jnp.int32, (8, 128), 1) < 8

    def totals(values):
        for i, value in enumerate(values):
            rows_ref[i : i + 1] = value
        summed = jnp.sum(jnp.where(slim, rows_ref[...], 0.0), axis=1, keepdims=True)
        rows_ref[...] = jnp.broadcast_to(summed, (8, 128))
        return [rows_ref[i : i + 1] for i in range(len(values))]

    l00, l01, l11, b00, b01, b11, u00, u01, u11, e00, e01, e11 = (
        pltpu.roll(total, (128 - 8 * i) % 128, 1) if i else total for i in range(12)
    )
    m00, m01, m11, h00, h11 = totals([l00, l01, l11, b00, b11])
    mu = [h00 / m00, h11 / m11]
    w00, w01, w11, e00, e01, e11, c01, c10 = totals(
        [
            u00 - mu[0] * (2.0 * b00 - mu[0] * l00),
            u01 - (mu[0] + mu[1]) * b01 + mu[0] * mu[1] * l01,
            u11 - mu[1] * (2.0 * b11 - mu[1] * l11),
            e00 - mu[0] * (2.0 * u00 - mu[0] * b00),
            e01 - (mu[0] + mu[1]) * u01 + mu[0] * mu[1] * b01,
            e11 - mu[1] * (2.0 * u11 - mu[1] * b11),
            b01 - mu[1] * l01,
            b01 - mu[0] * l01,
        ]
    )

    top = 1.5 * math.pi**2 + 3.0

    def factors(mean, norm, ww, whw):
        nu = jnp.where(ww > 0.0, jnp.clip(whw / jnp.where(ww > 0.0, ww, 1.0), 0.0, top), mean)
        t2 = jnp.maximum(ww, 0.0) / norm
        p, q = mean - 1.0, nu - 1.0
        trace, det = p + q, p * q - t2
        real, imag = det * det - 1.0, 2.0 * det - trace * trace
        size = real * real + imag * imag
        return ((det - q * trace) * imag - real) / size, trace * imag / size

    def gram(ref, upper, cross, lower):
        lane = lax.broadcasted_iota(jnp.int32, (1, 128), 1)
        ref[0:1, :] = jnp.where(lane == 0, upper, cross)[:, 0:2]
        ref[1:2, :] = jnp.where(lane == 0, cross, lower)[:, 0:2]

    a0, f0 = factors(mu[0], m00, w00, e00)
    a1, f1 = factors(mu[1], m11, w11, e11)
    first = pole == 0
    a, f = jnp.where(first, a0, a1), jnp.where(first, f0, f1)
    my_mu = jnp.where(first, mu[0], mu[1])
    column_block = lane_block(pole)
    for block, base, applied in (
        (lane_block(pole), own_b[:, :, column_block], u_ref[:, :, column_block]),
        (lane_block(partner), far_b[:, :, column_block], far_u[...]),
    ):
        out_ref[0, :, :, block] = a * base + f * (applied - my_mu * base)
    cross = a0 * a1 * m01 + a0 * f1 * c01 + f0 * a1 * c10 + f0 * f1 * w01
    gram(corr_ref, a0 * a0 * m00 + f0 * f0 * w00, cross, a1 * a1 * m11 + f1 * f1 * w11)
    cross = (
        a0 * a1 * (c01 + mu[1] * m01)
        + a0 * f1 * (w01 + mu[0] * c01)
        + f0 * a1 * (w01 + mu[1] * c10)
        + f0 * f1 * e01
    )
    gram(
        energy_ref,
        a0 * a0 * mu[0] * m00 + 2.0 * a0 * f0 * w00 + f0 * f0 * e00,
        cross,
        a1 * a1 * mu[1] * m11 + 2.0 * a1 * f1 * w11 + f1 * f1 * e11,
    )
    sent(parts, messages, 9)


def local(states, potential):
    columns, cy, cz, nx = states.shape
    fy, fz, poles = lax.axis_size("fy"), lax.axis_size("fz"), lax.axis_size("pole")
    half = nx // 2
    f32 = jnp.float32
    in_vmem = pl.BlockSpec(memory_space=pltpu.VMEM)
    in_hbm = pl.BlockSpec(memory_space=pl.ANY)

    def vmem(*shape):
        return pltpu.VMEM(shape, f32)

    x_block, y_block, z_block = vmem(cy, cz, nx), vmem(fy, cy, nx), vmem(fz, cz, nx)
    filtered, corr, energy = pl.pallas_call(
        functools.partial(kernel, cy, cz, nx, fy, fz, poles),
        out_shape=(
            jax.ShapeDtypeStruct((1, cy, cz, nx), f32),
            jax.ShapeDtypeStruct((columns, columns), f32),
            jax.ShapeDtypeStruct((columns, columns), f32),
        ),
        in_specs=[in_hbm] * 5,
        out_specs=(in_vmem,) * 3,
        scratch_shapes=[
            *[x_block] * 3,
            vmem(nx, nx), vmem(cy * fy, cy * fy), vmem(cz * fz, cz * fz),
            *[x_block] * 7, vmem(cy, cz, half),
            *[y_block] * 9,
            *[z_block] * 6,
            vmem(16, 128), vmem(1, 128), vmem(1, 128), vmem(1, 128), vmem(fy * poles * fz, 128), vmem(8, 128),
            pltpu.SemaphoreType.DMA((9,)),
            pltpu.SemaphoreType.DMA((11,)),
            pltpu.SemaphoreType.DMA((11,)),
        ],
        compiler_params=pltpu.CompilerParams(
            collective_id=0, has_side_effects=True, vmem_limit_bytes=32 * 1024 * 1024
        ),
    )(
        *(
            pltpu.with_memory_space_constraint(operand, pltpu.HBM)
            for operand in (
                states,
                potential,
                jnp.asarray(axis_operator(nx)),
                jnp.asarray(axis_operator(cy * fy)),
                jnp.asarray(axis_operator(cz * fz)),
            )
        )
    )
    cells = 1.0 / float(nx * cy * fy * cz * fz)
    return filtered, corr * cells, energy * cells


def solution(mesh):
    placed = (P(None, "fy", "fz", None), P("fy", "fz", None))
    return jax.shard_map(
        local,
        mesh=mesh,
        in_specs=placed,
        out_specs=(P("pole", "fy", "fz", None), P(), P()),
        check_vma=False,
    )
```

```python
import functools
import math

import jax
import jax.numpy as jnp
import numpy as np
from jax import lax
from jax.experimental import pallas as pl
from jax.experimental.pallas import tpu as pltpu
from jax.sharding import PartitionSpec as P

MESH = pl.DeviceIdType.MESH
HIGH = lax.Precision.HIGHEST


def axis_operator(length):
    index = np.arange(length)
    signed = np.where(index < length // 2, index, index - length) * (2.0 * math.pi / length)
    phases = (index[:, None] * index[None, :] % length) * (2.0 * math.pi / length)
    first = (np.cos(phases) @ (0.5 * signed * signed)) / length
    return np.asarray(first[(index[:, None] - index[None, :]) % length], np.float32)


def far_first(count):
    return sorted(range(1, count), key=lambda k: -min(k, count - k))


def dot(left, right):
    return jnp.dot(left, right, precision=HIGH, preferred_element_type=jnp.float32)


def lanes(product):
    return jnp.sum(product, axis=0, keepdims=True)


def kernel(
    cy, cz, nx, fy, fz, poles,
    states_hbm, pot_hbm, dx_hbm, dy_hbm, dz_hbm,
    out_ref, corr_ref, energy_ref,
    own_b, far_b, v_ref, dx_ref, dy_ref, dz_ref, g_ref, s_ref, q_ref, u_ref, y_ref, dxs_ref, dxg_ref, far_u,
    ysend, yb, ymul, ymul2, yback, yback2, vsend, yv, z_order, g_order,
    zb, zq, zmul, zmul2, zback, zback2,
    acc, mine_sums, core_sums, chip_sums, parts, rows_ref,
    load_sem, send_sem, recv_sem,
):
    pole, my, mz = lax.axis_index("pole"), lax.axis_index("fy"), lax.axis_index("fz")
    partner = 1 - pole
    rows = cy * cz
    half = nx // 2
    col0, col1 = slice(0, half), slice(half, nx)

    def lane_block(index):
        return pl.ds(pl.multiple_of(index * half, half), half)

    def at_y(step):
        return (pole, lax.rem(my + step, fy), mz)

    def at_z(step):
        return (pole, my, lax.rem(mz + step, fz))

    def push(src, dst, place, slot):
        pltpu.make_async_remote_copy(
            src_ref=src,
            dst_ref=dst,
            send_sem=send_sem.at[slot],
            recv_sem=recv_sem.at[slot],
            device_id=place,
            device_id_type=MESH,
        ).start()

    def push_y(src, dst, step, slot):
        push(src.at[lax.rem(my + step, fy)], dst.at[my], at_y(step), slot)

    def push_z(src, dst, step, slot):
        push(src.at[lax.rem(mz + step, fz)], dst.at[mz], at_z(step), slot)

    def scatter_y(src, dst, slot):
        for step in far_first(fy):
            push_y(src, dst, step, slot)
        dst[my] = src[my]

    def scatter_z(src, dst, slot):
        for step in far_first(fz):
            push_z(src, dst, step, slot)
        dst[mz] = src[mz]

    def arrived(dst, count, slot):
        whole = dst.at[pl.ds(0, count)]
        pltpu.make_async_copy(whole, whole, recv_sem.at[slot]).wait()

    def sent(dst, count, slot):
        whole = dst.at[pl.ds(0, count)]
        pltpu.make_async_copy(whole, whole, send_sem.at[slot]).wait()

    parts[...] = jnp.zeros(parts.shape, jnp.float32)
    barrier = pltpu.get_barrier_semaphore()

    for step in far_first(fy):
        pl.semaphore_signal(barrier, inc=1, device_id=at_y(step), device_id_type=MESH)
    for step in far_first(fz):
        pl.semaphore_signal(barrier, inc=1, device_id=at_z(step), device_id_type=MESH)
    across = (partner, my, mz)
    pl.semaphore_signal(barrier, inc=1, device_id=across, device_id_type=MESH)

    def load(src, dst, slot):
        copy = pltpu.make_async_copy(src, dst, load_sem.at[slot])
        copy.start()
        return copy

    near = [load(states_hbm.at[c, :, :, lane_block(pole)], own_b.at[:, :, pl.ds(c * half, half)], c) for c in range(2)]
    rest = [
        load(states_hbm.at[c, :, :, lane_block(partner)], far_b.at[:, :, pl.ds(c * half, half)], 2 + c) for c in range(2)
    ]
    rest.append(load(pot_hbm.at[:, :, lane_block(pole)], v_ref.at[:, :, pl.ds(0, half)], 4))
    rest.append(load(pot_hbm.at[:, :, lane_block(partner)], v_ref.at[:, :, pl.ds(half, half)], 5))
    rest.append(load(dx_hbm, dx_ref, 6))
    rest.append(load(dz_hbm, dz_ref, 7))
    rest.append(load(dy_hbm, dy_ref, 8))
    for copy in near:
        copy.wait()
    for c in range(2):
        ysend[c] = jnp.swapaxes(own_b[:, :, c * half : (c + 1) * half], 0, 1)
    for copy in rest:
        copy.wait()

    def flat(ref):
        return ref[...].reshape(rows, nx)

    def column(ref, c):
        return ref[:, :, c * half : (c + 1) * half].reshape(-1, half)

    terms = [jnp.zeros((1, half), jnp.float32)] * 3

    def quadratic(left, right):
        terms[0] += lanes(left[0] * right[0])
        terms[1] += lanes(left[0] * right[1])
        terms[2] += lanes(left[1] * right[1])

    def symmetric(left, right):
        terms[0] += 2.0 * lanes(left[0] * right[0])
        terms[1] += lanes(left[0] * right[1] + left[1] * right[0])
        terms[2] += 2.0 * lanes(left[1] * right[1])

    v = v_ref[...].reshape(rows, nx)
    b = [column(own_b, c) for c in range(2)]
    g, s = [], []
    for c in range(2):
        whole = jnp.concatenate([b[c], column(far_b, c)], axis=1)
        g.append(dot(whole, dx_ref[...]))
        s.append(v * whole + g[c])
        here = slice(c * half, (c + 1) * half)
        s_ref[:, :, here] = s[c][:, col0].reshape(cy, cz, half)
        g_ref[:, :, here] = g[c][:, col0].reshape(cy, cz, half)
        q_ref[:, :, here] = (s[c][:, col0] + 0.5 * g[c][:, col0]).reshape(cy, cz, half)
    vsend[...] = jnp.swapaxes(v_ref[:, :, 0:half], 0, 1)
    g_order[...] = jnp.swapaxes(g_ref[...], 0, 1)

    pl.semaphore_wait(barrier, fy + fz - 1)
    scatter_y(ysend.at[0], yb.at[0], 0)
    scatter_y(ysend.at[1], yb.at[1], 11)
    scatter_z(own_b, zb, 1)
    scatter_y(vsend, yv, 2)
    scatter_z(q_ref, zq, 3)

    acc[0:1] = lanes(b[0] * b[0])
    acc[1:2] = lanes(b[0] * b[1])
    acc[2:3] = lanes(b[1] * b[1])
    acc[12:16] = jnp.zeros((4, 128), jnp.float32)
    for c in range(2):
        here = slice(c * half, (c + 1) * half)
        dxs_ref[:, :, here] = dot(s[c], dx_ref[:, col0]).reshape(cy, cz, half)
        dxg_ref[:, :, here] = dot(g[c], dx_ref[:, col0]).reshape(cy, cz, half)
    quadratic([s[c][:, col0] for c in range(2)], [column(dxs_ref, c) for c in range(2)])

    def y_column(c, slot, slot2):
        ymul[c] = dot(dy_ref[...], yb[c].reshape(-1, half)).reshape(fy, cy, half)
        ymul2[c] = dot(dy_ref[...], ymul[c].reshape(-1, half)).reshape(fy, cy, half)
        for step in far_first(fy):
            push_y(ymul.at[c], yback.at[c], step, slot)
            push_y(ymul2.at[c], yback2.at[c], step, slot2)
        yback[c, my] = ymul[c, my]
        yback2[c, my] = ymul2[c, my]

    arrived(yb.at[0], fy - 1, 0)
    y_column(0, 4, 6)
    arrived(yb.at[1], fy - 1, 11)
    y_column(1, 12, 13)
    arrived(zb, fz - 1, 1)
    zmul[...] = dot(dz_ref[...], flat(zb)).reshape(fz, cz, nx)
    scatter_z(zmul, zback, 5)
    z_twice = dot(dz_ref[...], flat(zmul))
    arrived(zq, fz - 1, 3)
    p = flat(zq) + flat(zmul)
    p_mul = dot(dz_ref[...], p)
    zmul2[...] = (4.0 * p_mul - z_twice).reshape(fz, cz, nx)
    scatter_z(zmul2, zback2, 7)
    quadratic([p[:, col0], p[:, col1]], [p_mul[:, col0], p_mul[:, col1]])
    arrived(yv, fy - 1, 2)
    h = [(yv[...] * yb[c]).reshape(-1, half) for c in range(2)]
    p_mul = [dot(dy_ref[...], h[c]) + ymul2[c].reshape(-1, half) for c in range(2)]
    quadratic([h[c] + ymul[c].reshape(-1, half) for c in range(2)], p_mul)

    arrived(zback, fz - 1, 5)
    for c, slot in ((0, 4), (1, 12)):
        arrived(yback.at[c], fy - 1, slot)
        y_ref[:, :, c * half : (c + 1) * half] = jnp.swapaxes(yback[c], 0, 1)
    u_ref[...] = s_ref[...] + zback[...] + y_ref[...]
    push(u_ref.at[:, :, lane_block(partner)], far_u, across, 10)
    u = [column(u_ref, c) for c in range(2)]
    acc[3:4] = lanes(b[0] * u[0])
    acc[4:5] = lanes(b[0] * u[1])
    acc[5:6] = lanes(b[1] * u[1])
    acc[6:7] = lanes(u[0] * u[0])
    acc[7:8] = lanes(u[0] * u[1])
    acc[8:9] = lanes(u[1] * u[1])
    quadratic(u, [v[:, col0] * u[c] for c in range(2)])
    y = [column(y_ref, c) for c in range(2)]
    symmetric([2.0 * column(dxs_ref, c) - 0.5 * column(dxg_ref, c) for c in range(2)], y)
    symmetric(
        [0.5 * column(dxs_ref, c) - 0.125 * column(dxg_ref, c) for c in range(2)],
        [column(zback, c) for c in range(2)],
    )
    z_order[...] = 1.5 * (g_order[...] + jnp.swapaxes(zback[...], 0, 1))
    arrived(zback2, fz - 1, 7)
    symmetric([0.5 * y[c] for c in range(2)], [column(zback2, c) for c in range(2)])
    for c, slot in ((0, 6), (1, 13)):
        arrived(yback2.at[c], fy - 1, slot)
    symmetric([column(z_order, c) for c in range(2)], [yback2[c].reshape(-1, half) for c in range(2)])
    for i in range(3):
        acc[9 + i : 10 + i] = terms[i]

    lane = lax.broadcasted_iota(jnp.int32, (16, 128), 1)
    row = lax.broadcasted_iota(jnp.int32, (16, 128), 0)
    folded = acc[...]
    for shift in (64, 32, 16, 8):
        folded = folded + pltpu.roll(folded, shift, 1)
    mine_sums[...] = jnp.sum(jnp.where(lane // 8 == row, folded, 0.0), axis=0, keepdims=True)

    core = lax.rem(mz, 2)
    push(mine_sums, core_sums, (pole, my, mz + 1 - 2 * core), 8)
    size_x, size_y = 2 * poles, fz // 4
    place_x = [lax.rem(2 * pole + lax.rem(mz // 2, 2) + k, size_x) for k in range(size_x)]
    place_y = [lax.rem(mz // 4 + k, size_y) for k in range(size_y)]
    place_z = [lax.rem(my + k, fy) for k in range(fy)]
    pole_of = [x // 2 for x in place_x]
    low_of = [2 * lax.rem(x, 2) for x in place_x]
    chip = (my * size_y + mz // 4) * size_x + place_x[0]

    def hops(offset):
        return sum(min(k, n - k) for k, n in zip(offset, (size_x, size_y, fy)))

    offsets = sorted(
        ((x, y, z) for x in range(size_x) for y in range(size_y) for z in range(fy) if (x, y, z) != (0, 0, 0)),
        key=lambda offset: -hops(offset),
    )
    far_away = [offset for offset in offsets if hops(offset) >= hops(offsets[0]) - 3]

    def device(offset, which):
        x, y, z = offset
        return (pole_of[x], place_z[z], place_y[y] * 4 + low_of[x] + which)

    chips = size_x * size_y * fy
    mine_row = pl.ds(core * chips + chip, 1)
    pair_row = pl.ds(chip, 1)
    for offset in far_away:
        for which in range(2):
            push(mine_sums, parts.at[mine_row], device(offset, which), 9)

    whole_core = core_sums.at[pl.ds(0, 1)]
    pltpu.make_async_copy(whole_core, whole_core, recv_sem.at[8]).wait()
    chip_sums[...] = mine_sums[...] + core_sums[...]
    for offset in offsets[len(far_away) :]:
        push(chip_sums, parts.at[pair_row], device(offset, core), 9)
    parts[pair_row, :] = chip_sums[...]
    messages = len(offsets) + len(far_away)

    for slot, z_buffer in ((1, zb), (3, zq), (5, zback), (7, zback2)):
        sent(z_buffer, fz - 1, slot)
    for y_buffer, slots in ((yb, (0, 11)), (yback, (4, 12)), (yback2, (6, 13))):
        for c in range(2):
            sent(y_buffer.at[c], fy - 1, slots[c])
    sent(yv, fy - 1, 2)
    arrived(far_u, cy, 10)
    sent(far_u, cy, 10)
    pltpu.make_async_copy(whole_core, whole_core, send_sem.at[8]).wait()

    arrived(parts, messages, 9)
    total = jnp.sum(parts[0:chips] + parts[chips : 2 * chips], axis=0, keepdims=True)
    slim = lax.broadcasted_iota(jnp.int32, (8, 128), 1) < 8

    def totals(values):
        for i, value in enumerate(values):
            rows_ref[i : i + 1] = value
        summed = jnp.sum(jnp.where(slim, rows_ref[...], 0.0), axis=1, keepdims=True)
        rows_ref[...] = jnp.broadcast_to(summed, (8, 128))
        return [rows_ref[i : i + 1] for i in range(len(values))]

    l00, l01, l11, b00, b01, b11, u00, u01, u11, e00, e01, e11 = (
        pltpu.roll(total, (128 - 8 * i) % 128, 1) if i else total for i in range(12)
    )
    m00, m01, m11, h00, h11 = totals([l00, l01, l11, b00, b11])
    mu = [h00 / m00, h11 / m11]
    w00, w01, w11, e00, e01, e11, c01, c10 = totals(
        [
            u00 - mu[0] * (2.0 * b00 - mu[0] * l00),
            u01 - (mu[0] + mu[1]) * b01 + mu[0] * mu[1] * l01,
            u11 - mu[1] * (2.0 * b11 - mu[1] * l11),
            e00 - mu[0] * (2.0 * u00 - mu[0] * b00),
            e01 - (mu[0] + mu[1]) * u01 + mu[0] * mu[1] * b01,
            e11 - mu[1] * (2.0 * u11 - mu[1] * b11),
            b01 - mu[1] * l01,
            b01 - mu[0] * l01,
        ]
    )

    top = 1.5 * math.pi**2 + 3.0

    def factors(mean, norm, ww, whw):
        nu = jnp.where(ww > 0.0, jnp.clip(whw / jnp.where(ww > 0.0, ww, 1.0), 0.0, top), mean)
        t2 = jnp.maximum(ww, 0.0) / norm
        p, q = mean - 1.0, nu - 1.0
        trace, det = p + q, p * q - t2
        real, imag = det * det - 1.0, 2.0 * det - trace * trace
        size = real * real + imag * imag
        return ((det - q * trace) * imag - real) / size, trace * imag / size

    def gram(ref, upper, cross, lower):
        lane = lax.broadcasted_iota(jnp.int32, (1, 128), 1)
        ref[0:1, :] = jnp.where(lane == 0, upper, cross)[:, 0:2]
        ref[1:2, :] = jnp.where(lane == 0, cross, lower)[:, 0:2]

    a0, f0 = factors(mu[0], m00, w00, e00)
    a1, f1 = factors(mu[1], m11, w11, e11)
    first = pole == 0
    a, f = jnp.where(first, a0, a1), jnp.where(first, f0, f1)
    my_mu = jnp.where(first, mu[0], mu[1])
    column_block = lane_block(pole)
    for block, base, applied in (
        (lane_block(pole), own_b[:, :, column_block], u_ref[:, :, column_block]),
        (lane_block(partner), far_b[:, :, column_block], far_u[...]),
    ):
        out_ref[0, :, :, block] = a * base + f * (applied - my_mu * base)
    cross = a0 * a1 * m01 + a0 * f1 * c01 + f0 * a1 * c10 + f0 * f1 * w01
    gram(corr_ref, a0 * a0 * m00 + f0 * f0 * w00, cross, a1 * a1 * m11 + f1 * f1 * w11)
    cross = (
        a0 * a1 * (c01 + mu[1] * m01)
        + a0 * f1 * (w01 + mu[0] * c01)
        + f0 * a1 * (w01 + mu[1] * c10)
        + f0 * f1 * e01
    )
    gram(
        energy_ref,
        a0 * a0 * mu[0] * m00 + 2.0 * a0 * f0 * w00 + f0 * f0 * e00,
        cross,
        a1 * a1 * mu[1] * m11 + 2.0 * a1 * f1 * w11 + f1 * f1 * e11,
    )
    sent(parts, messages, 9)


def local(states, potential):
    columns, cy, cz, nx = states.shape
    fy, fz, poles = lax.axis_size("fy"), lax.axis_size("fz"), lax.axis_size("pole")
    half = nx // 2
    f32 = jnp.float32
    in_vmem = pl.BlockSpec(memory_space=pltpu.VMEM)
    in_hbm = pl.BlockSpec(memory_space=pl.ANY)

    def vmem(*shape):
        return pltpu.VMEM(shape, f32)

    x_block, y_block, z_block = vmem(cy, cz, nx), vmem(fy, cy, nx), vmem(fz, cz, nx)
    filtered, corr, energy = pl.pallas_call(
        functools.partial(kernel, cy, cz, nx, fy, fz, poles),
        out_shape=(
            jax.ShapeDtypeStruct((1, cy, cz, nx), f32),
            jax.ShapeDtypeStruct((columns, columns), f32),
            jax.ShapeDtypeStruct((columns, columns), f32),
        ),
        in_specs=[in_hbm] * 5,
        out_specs=(in_vmem,) * 3,
        scratch_shapes=[
            *[x_block] * 3,
            vmem(nx, nx), vmem(cy * fy, cy * fy), vmem(cz * fz, cz * fz),
            *[x_block] * 7, vmem(cy, cz, half),
            *[vmem(columns, fy, cy, half)] * 6, vmem(fy, cy, half), vmem(fy, cy, half), y_block, y_block,
            *[z_block] * 6,
            vmem(16, 128), vmem(1, 128), vmem(1, 128), vmem(1, 128), vmem(fy * poles * fz, 128), vmem(8, 128),
            pltpu.SemaphoreType.DMA((9,)),
            pltpu.SemaphoreType.DMA((14,)),
            pltpu.SemaphoreType.DMA((14,)),
        ],
        compiler_params=pltpu.CompilerParams(
            collective_id=0, has_side_effects=True, vmem_limit_bytes=32 * 1024 * 1024
        ),
    )(
        *(
            pltpu.with_memory_space_constraint(operand, pltpu.HBM)
            for operand in (
                states,
                potential,
                jnp.asarray(axis_operator(nx)),
                jnp.asarray(axis_operator(cy * fy)),
                jnp.asarray(axis_operator(cz * fz)),
            )
        )
    )
    cells = 1.0 / float(nx * cy * fy * cz * fz)
    return filtered, corr * cells, energy * cells


def solution(mesh):
    placed = (P(None, "fy", "fz", None), P("fy", "fz", None))
    return jax.shard_map(
        local,
        mesh=mesh,
        in_specs=placed,
        out_specs=(P("pole", "fy", "fz", None), P(), P()),
        check_vma=False,
    )
```

```python
import functools
import math

import jax
import jax.numpy as jnp
import numpy as np
from jax import lax
from jax.experimental import pallas as pl
from jax.experimental.pallas import tpu as pltpu
from jax.sharding import PartitionSpec as P

MESH = pl.DeviceIdType.MESH
HIGH = lax.Precision.HIGHEST


def axis_operator(length):
    index = np.arange(length)
    signed = np.where(index < length // 2, index, index - length) * (2.0 * math.pi / length)
    phases = (index[:, None] * index[None, :] % length) * (2.0 * math.pi / length)
    first = (np.cos(phases) @ (0.5 * signed * signed)) / length
    return np.asarray(first[(index[:, None] - index[None, :]) % length], np.float32)


def far_first(count):
    return sorted(range(1, count), key=lambda k: -min(k, count - k))


def dot(left, right):
    return jnp.dot(left, right, precision=HIGH, preferred_element_type=jnp.float32)


def lanes(product):
    return jnp.sum(product, axis=0, keepdims=True)


def kernel(
    cy, cz, nx, fy, fz, poles,
    states_hbm, pot_hbm, dx_hbm, dy_hbm, dz_hbm,
    out_ref, corr_ref, energy_ref,
    own_b, far_b, v_ref, dx_ref, dy_ref, dz_ref, g_ref, s_ref, q_ref, u_ref, y_ref, dxs_ref, dxg_ref, far_u,
    ysend, yb, ymul, ymul2, yback, yback2, vsend, yv, z_order, g_order,
    zb, zq, zmul, zmul2, zback, zback2,
    acc, mine_sums, core_sums, chip_sums, parts, rows_ref,
    load_sem, send_sem, recv_sem,
):
    pole, my, mz = lax.axis_index("pole"), lax.axis_index("fy"), lax.axis_index("fz")
    partner = 1 - pole
    rows = cy * cz
    half = nx // 2
    col0, col1 = slice(0, half), slice(half, nx)

    def lane_block(index):
        return pl.ds(pl.multiple_of(index * half, half), half)

    def at_y(step):
        return (pole, lax.rem(my + step, fy), mz)

    def at_z(step):
        return (pole, my, lax.rem(mz + step, fz))

    def push(src, dst, place, slot):
        pltpu.make_async_remote_copy(
            src_ref=src,
            dst_ref=dst,
            send_sem=send_sem.at[slot],
            recv_sem=recv_sem.at[slot],
            device_id=place,
            device_id_type=MESH,
        ).start()

    def push_y(src, dst, step, slot):
        push(src.at[lax.rem(my + step, fy)], dst.at[my], at_y(step), slot)

    def push_z(src, dst, step, slot):
        push(src.at[lax.rem(mz + step, fz)], dst.at[mz], at_z(step), slot)

    def scatter_y(src, dst, slot):
        for step in far_first(fy):
            push_y(src, dst, step, slot)
        dst[my] = src[my]

    def scatter_z(src, dst, slot):
        for step in far_first(fz):
            push_z(src, dst, step, slot)
        dst[mz] = src[mz]

    def arrived(dst, count, slot):
        whole = dst.at[pl.ds(0, count)]
        pltpu.make_async_copy(whole, whole, recv_sem.at[slot]).wait()

    def sent(dst, count, slot):
        whole = dst.at[pl.ds(0, count)]
        pltpu.make_async_copy(whole, whole, send_sem.at[slot]).wait()

    parts[...] = jnp.zeros(parts.shape, jnp.float32)
    barrier = pltpu.get_barrier_semaphore()

    for step in far_first(fy):
        pl.semaphore_signal(barrier, inc=1, device_id=at_y(step), device_id_type=MESH)
    for step in far_first(fz):
        pl.semaphore_signal(barrier, inc=1, device_id=at_z(step), device_id_type=MESH)
    across = (partner, my, mz)
    pl.semaphore_signal(barrier, inc=1, device_id=across, device_id_type=MESH)

    def load(src, dst, slot):
        copy = pltpu.make_async_copy(src, dst, load_sem.at[slot])
        copy.start()
        return copy

    near = [load(states_hbm.at[c, :, :, lane_block(pole)], own_b.at[:, :, pl.ds(c * half, half)], c) for c in range(2)]
    rest = [
        load(states_hbm.at[c, :, :, lane_block(partner)], far_b.at[:, :, pl.ds(c * half, half)], 2 + c) for c in range(2)
    ]
    rest.append(load(pot_hbm.at[:, :, lane_block(pole)], v_ref.at[:, :, pl.ds(0, half)], 4))
    rest.append(load(pot_hbm.at[:, :, lane_block(partner)], v_ref.at[:, :, pl.ds(half, half)], 5))
    rest.append(load(dx_hbm, dx_ref, 6))
    rest.append(load(dz_hbm, dz_ref, 7))
    rest.append(load(dy_hbm, dy_ref, 8))
    for copy in near:
        copy.wait()
    for c in range(2):
        ysend[c] = jnp.swapaxes(own_b[:, :, c * half : (c + 1) * half], 0, 1)
    for copy in rest:
        copy.wait()

    def flat(ref):
        return ref[...].reshape(rows, nx)

    def column(ref, c):
        return ref[:, :, c * half : (c + 1) * half].reshape(-1, half)

    terms = [jnp.zeros((1, half), jnp.float32)] * 3

    def quadratic(left, right):
        terms[0] += lanes(left[0] * right[0])
        terms[1] += lanes(left[0] * right[1])
        terms[2] += lanes(left[1] * right[1])

    def symmetric(left, right):
        terms[0] += 2.0 * lanes(left[0] * right[0])
        terms[1] += lanes(left[0] * right[1] + left[1] * right[0])
        terms[2] += 2.0 * lanes(left[1] * right[1])

    v = v_ref[...].reshape(rows, nx)
    b = [column(own_b, c) for c in range(2)]
    g, s = [], []
    for c in range(2):
        whole = jnp.concatenate([b[c], column(far_b, c)], axis=1)
        g.append(dot(whole, dx_ref[...]))
        s.append(v * whole + g[c])
        here = slice(c * half, (c + 1) * half)
        s_ref[:, :, here] = s[c][:, col0].reshape(cy, cz, half)
        g_ref[:, :, here] = g[c][:, col0].reshape(cy, cz, half)
        q_ref[:, :, here] = (s[c][:, col0] + 0.5 * g[c][:, col0]).reshape(cy, cz, half)
    vsend[...] = jnp.swapaxes(v_ref[:, :, 0:half], 0, 1)
    g_order[...] = jnp.swapaxes(g_ref[...], 0, 1)

    pl.semaphore_wait(barrier, fy + fz - 1)
    scatter_y(ysend.at[0], yb.at[0], 0)
    scatter_y(ysend.at[1], yb.at[1], 11)
    scatter_z(own_b, zb, 1)
    scatter_y(vsend, yv, 2)
    scatter_z(q_ref, zq, 3)

    acc[0:1] = lanes(b[0] * b[0])
    acc[1:2] = lanes(b[0] * b[1])
    acc[2:3] = lanes(b[1] * b[1])
    acc[12:16] = jnp.zeros((4, 128), jnp.float32)
    for c in range(2):
        here = slice(c * half, (c + 1) * half)
        dxs_ref[:, :, here] = dot(s[c], dx_ref[:, col0]).reshape(cy, cz, half)
        dxg_ref[:, :, here] = dot(g[c], dx_ref[:, col0]).reshape(cy, cz, half)
    quadratic([s[c][:, col0] for c in range(2)], [column(dxs_ref, c) for c in range(2)])

    def y_column(c, slot, slot2):
        ymul[c] = dot(dy_ref[...], yb[c].reshape(-1, half)).reshape(fy, cy, half)
        ymul2[c] = dot(dy_ref[...], ymul[c].reshape(-1, half)).reshape(fy, cy, half)
        for step in far_first(fy):
            push_y(ymul.at[c], yback.at[c], step, slot)
            push_y(ymul2.at[c], yback2.at[c], step, slot2)
        yback[c, my] = ymul[c, my]
        yback2[c, my] = ymul2[c, my]

    arrived(yb.at[0], fy - 1, 0)
    y_column(0, 4, 6)
    arrived(yb.at[1], fy - 1, 11)
    y_column(1, 12, 13)
    arrived(zb, fz - 1, 1)
    zmul[...] = dot(dz_ref[...], flat(zb)).reshape(fz, cz, nx)
    scatter_z(zmul, zback, 5)
    z_twice = dot(dz_ref[...], flat(zmul))
    arrived(zq, fz - 1, 3)
    p = flat(zq) + flat(zmul)
    p_mul = dot(dz_ref[...], p)
    zmul2[...] = (4.0 * p_mul - z_twice).reshape(fz, cz, nx)
    scatter_z(zmul2, zback2, 7)
    quadratic([p[:, col0], p[:, col1]], [p_mul[:, col0], p_mul[:, col1]])
    arrived(yv, fy - 1, 2)
    h = [(yv[...] * yb[c]).reshape(-1, half) for c in range(2)]
    p_mul = [dot(dy_ref[...], h[c]) + ymul2[c].reshape(-1, half) for c in range(2)]
    quadratic([h[c] + ymul[c].reshape(-1, half) for c in range(2)], p_mul)

    arrived(zback, fz - 1, 5)
    for c, slot in ((0, 4), (1, 12)):
        arrived(yback.at[c], fy - 1, slot)
        y_ref[:, :, c * half : (c + 1) * half] = jnp.swapaxes(yback[c], 0, 1)
    u_ref[...] = s_ref[...] + zback[...] + y_ref[...]
    push(u_ref.at[:, :, lane_block(partner)], far_u, across, 10)
    u = [column(u_ref, c) for c in range(2)]
    acc[3:4] = lanes(b[0] * u[0])
    acc[4:5] = lanes(b[0] * u[1])
    acc[5:6] = lanes(b[1] * u[1])
    acc[6:7] = lanes(u[0] * u[0])
    acc[7:8] = lanes(u[0] * u[1])
    acc[8:9] = lanes(u[1] * u[1])
    quadratic(u, [v[:, col0] * u[c] for c in range(2)])
    y = [column(y_ref, c) for c in range(2)]
    symmetric([2.0 * column(dxs_ref, c) - 0.5 * column(dxg_ref, c) for c in range(2)], y)
    symmetric(
        [0.5 * column(dxs_ref, c) - 0.125 * column(dxg_ref, c) for c in range(2)],
        [column(zback, c) for c in range(2)],
    )
    z_order[...] = 1.5 * (g_order[...] + jnp.swapaxes(zback[...], 0, 1))
    arrived(zback2, fz - 1, 7)
    symmetric([0.5 * y[c] for c in range(2)], [column(zback2, c) for c in range(2)])
    for c, slot in ((0, 6), (1, 13)):
        arrived(yback2.at[c], fy - 1, slot)
    symmetric([column(z_order, c) for c in range(2)], [yback2[c].reshape(-1, half) for c in range(2)])
    for i in range(3):
        acc[9 + i : 10 + i] = terms[i]

    lane = lax.broadcasted_iota(jnp.int32, (16, 128), 1)
    row = lax.broadcasted_iota(jnp.int32, (16, 128), 0)
    folded = acc[...]
    for shift in (64, 32, 16, 8):
        folded = folded + pltpu.roll(folded, shift, 1)
    mine_sums[...] = jnp.sum(jnp.where(lane // 8 == row, folded, 0.0), axis=0, keepdims=True)

    core = lax.rem(mz, 2)
    push(mine_sums, core_sums, (pole, my, mz + 1 - 2 * core), 8)
    size_x, size_y = 2 * poles, fz // 4
    place_x = [lax.rem(2 * pole + lax.rem(mz // 2, 2) + k, size_x) for k in range(size_x)]
    place_y = [lax.rem(mz // 4 + k, size_y) for k in range(size_y)]
    place_z = [lax.rem(my + k, fy) for k in range(fy)]
    pole_of = [x // 2 for x in place_x]
    low_of = [2 * lax.rem(x, 2) for x in place_x]
    chip = (my * size_y + mz // 4) * size_x + place_x[0]

    def hops(offset):
        return sum(min(k, n - k) for k, n in zip(offset, (size_x, size_y, fy)))

    offsets = sorted(
        ((x, y, z) for x in range(size_x) for y in range(size_y) for z in range(fy) if (x, y, z) != (0, 0, 0)),
        key=lambda offset: -hops(offset),
    )
    far_away = [offset for offset in offsets if hops(offset) >= hops(offsets[0]) - 3]

    def device(offset, which):
        x, y, z = offset
        return (pole_of[x], place_z[z], place_y[y] * 4 + low_of[x] + which)

    chips = size_x * size_y * fy
    mine_row = pl.ds(core * chips + chip, 1)
    pair_row = pl.ds(chip, 1)
    for offset in far_away:
        for which in range(2):
            push(mine_sums, parts.at[mine_row], device(offset, which), 9)

    whole_core = core_sums.at[pl.ds(0, 1)]
    pltpu.make_async_copy(whole_core, whole_core, recv_sem.at[8]).wait()
    chip_sums[...] = mine_sums[...] + core_sums[...]
    for offset in offsets[len(far_away) :]:
        push(chip_sums, parts.at[pair_row], device(offset, core), 9)
    parts[pair_row, :] = chip_sums[...]
    messages = len(offsets) + len(far_away)

    for slot, z_buffer in ((1, zb), (3, zq), (5, zback), (7, zback2)):
        sent(z_buffer, fz - 1, slot)
    for y_buffer, slots in ((yb, (0, 11)), (yback, (4, 12)), (yback2, (6, 13))):
        for c in range(2):
            sent(y_buffer.at[c], fy - 1, slots[c])
    sent(yv, fy - 1, 2)
    arrived(far_u, cy, 10)
    sent(far_u, cy, 10)
    pltpu.make_async_copy(whole_core, whole_core, send_sem.at[8]).wait()

    arrived(parts, messages, 9)
    total = jnp.sum(parts[0:chips] + parts[chips : 2 * chips], axis=0, keepdims=True)
    slim = lax.broadcasted_iota(jnp.int32, (8, 128), 1) < 8

    def totals(values):
        for i, value in enumerate(values):
            rows_ref[i : i + 1] = value
        summed = jnp.sum(jnp.where(slim, rows_ref[...], 0.0), axis=1, keepdims=True)
        rows_ref[...] = jnp.broadcast_to(summed, (8, 128))
        return [rows_ref[i : i + 1] for i in range(len(values))]

    l00, l01, l11, b00, b01, b11, u00, u01, u11, e00, e01, e11 = (
        pltpu.roll(total, (128 - 8 * i) % 128, 1) if i else total for i in range(12)
    )
    m00, m01, m11, h00, h11 = totals([l00, l01, l11, b00, b11])
    mu = [h00 / m00, h11 / m11]
    w00, w01, w11, e00, e01, e11, c01, c10 = totals(
        [
            u00 - mu[0] * (2.0 * b00 - mu[0] * l00),
            u01 - (mu[0] + mu[1]) * b01 + mu[0] * mu[1] * l01,
            u11 - mu[1] * (2.0 * b11 - mu[1] * l11),
            e00 - mu[0] * (2.0 * u00 - mu[0] * b00),
            e01 - (mu[0] + mu[1]) * u01 + mu[0] * mu[1] * b01,
            e11 - mu[1] * (2.0 * u11 - mu[1] * b11),
            b01 - mu[1] * l01,
            b01 - mu[0] * l01,
        ]
    )

    top = 1.5 * math.pi**2 + 3.0

    def factors(mean, norm, ww, whw):
        nu = jnp.where(ww > 0.0, jnp.clip(whw / jnp.where(ww > 0.0, ww, 1.0), 0.0, top), mean)
        t2 = jnp.maximum(ww, 0.0) / norm
        p, q = mean - 1.0, nu - 1.0
        trace, det = p + q, p * q - t2
        real, imag = det * det - 1.0, 2.0 * det - trace * trace
        size = real * real + imag * imag
        return ((det - q * trace) * imag - real) / size, trace * imag / size

    per_cell = 1.0 / float(nx * cy * fy * cz * fz)

    def gram(ref, upper, cross, lower):
        lane = lax.broadcasted_iota(jnp.int32, (1, 128), 1)
        ref[0:1, :] = (jnp.where(lane == 0, upper, cross) * per_cell)[:, 0:2]
        ref[1:2, :] = (jnp.where(lane == 0, cross, lower) * per_cell)[:, 0:2]

    a0, f0 = factors(mu[0], m00, w00, e00)
    a1, f1 = factors(mu[1], m11, w11, e11)
    first = pole == 0
    a, f = jnp.where(first, a0, a1), jnp.where(first, f0, f1)
    my_mu = jnp.where(first, mu[0], mu[1])
    column_block = lane_block(pole)
    for block, base, applied in (
        (lane_block(pole), own_b[:, :, column_block], u_ref[:, :, column_block]),
        (lane_block(partner), far_b[:, :, column_block], far_u[...]),
    ):
        out_ref[0, :, :, block] = a * base + f * (applied - my_mu * base)
    cross = a0 * a1 * m01 + a0 * f1 * c01 + f0 * a1 * c10 + f0 * f1 * w01
    gram(corr_ref, a0 * a0 * m00 + f0 * f0 * w00, cross, a1 * a1 * m11 + f1 * f1 * w11)
    cross = (
        a0 * a1 * (c01 + mu[1] * m01)
        + a0 * f1 * (w01 + mu[0] * c01)
        + f0 * a1 * (w01 + mu[1] * c10)
        + f0 * f1 * e01
    )
    gram(
        energy_ref,
        a0 * a0 * mu[0] * m00 + 2.0 * a0 * f0 * w00 + f0 * f0 * e00,
        cross,
        a1 * a1 * mu[1] * m11 + 2.0 * a1 * f1 * w11 + f1 * f1 * e11,
    )
    sent(parts, messages, 9)


def local(states, potential):
    columns, cy, cz, nx = states.shape
    fy, fz, poles = lax.axis_size("fy"), lax.axis_size("fz"), lax.axis_size("pole")
    half = nx // 2
    f32 = jnp.float32
    in_vmem = pl.BlockSpec(memory_space=pltpu.VMEM)
    in_hbm = pl.BlockSpec(memory_space=pl.ANY)

    def vmem(*shape):
        return pltpu.VMEM(shape, f32)

    x_block, y_block, z_block = vmem(cy, cz, nx), vmem(fy, cy, nx), vmem(fz, cz, nx)
    filtered, corr, energy = pl.pallas_call(
        functools.partial(kernel, cy, cz, nx, fy, fz, poles),
        out_shape=(
            jax.ShapeDtypeStruct((1, cy, cz, nx), f32),
            jax.ShapeDtypeStruct((columns, columns), f32),
            jax.ShapeDtypeStruct((columns, columns), f32),
        ),
        in_specs=[in_hbm] * 5,
        out_specs=(in_vmem,) * 3,
        scratch_shapes=[
            *[x_block] * 3,
            vmem(nx, nx), vmem(cy * fy, cy * fy), vmem(cz * fz, cz * fz),
            *[x_block] * 7, vmem(cy, cz, half),
            *[vmem(columns, fy, cy, half)] * 6, vmem(fy, cy, half), vmem(fy, cy, half), y_block, y_block,
            *[z_block] * 6,
            vmem(16, 128), vmem(1, 128), vmem(1, 128), vmem(1, 128), vmem(fy * poles * fz, 128), vmem(8, 128),
            pltpu.SemaphoreType.DMA((9,)),
            pltpu.SemaphoreType.DMA((14,)),
            pltpu.SemaphoreType.DMA((14,)),
        ],
        compiler_params=pltpu.CompilerParams(
            collective_id=0, has_side_effects=True, vmem_limit_bytes=32 * 1024 * 1024
        ),
    )(
        *(
            pltpu.with_memory_space_constraint(operand, pltpu.HBM)
            for operand in (
                states,
                potential,
                jnp.asarray(axis_operator(nx)),
                jnp.asarray(axis_operator(cy * fy)),
                jnp.asarray(axis_operator(cz * fz)),
            )
        )
    )
    outs = (filtered, corr, energy)
    return pl.pallas_call(
        store,
        out_shape=tuple(jax.ShapeDtypeStruct(out.shape, f32) for out in outs),
        in_specs=[in_vmem] * 3,
        out_specs=(in_hbm,) * 3,
        scratch_shapes=[pltpu.SemaphoreType.DMA((3,))],
    )(*(pltpu.with_memory_space_constraint(out, pltpu.VMEM) for out in outs))


def store(filtered, corr, energy, filtered_out, corr_out, energy_out, sem):
    pairs = ((filtered, filtered_out), (corr, corr_out), (energy, energy_out))
    copies = [pltpu.make_async_copy(src, dst, sem.at[i]) for i, (src, dst) in enumerate(pairs)]
    for copy in copies:
        copy.start()
    for copy in copies:
        copy.wait()


def solution(mesh):
    placed = (P(None, "fy", "fz", None), P("fy", "fz", None))
    return jax.shard_map(
        local,
        mesh=mesh,
        in_specs=placed,
        out_specs=(P("pole", "fy", "fz", None), P(), P()),
        check_vma=False,
    )
```

```python
import functools
import math

import jax
import jax.numpy as jnp
import numpy as np
from jax import lax
from jax.experimental import pallas as pl
from jax.experimental.pallas import tpu as pltpu
from jax.sharding import PartitionSpec as P

MESH = pl.DeviceIdType.MESH
HIGH = lax.Precision.HIGHEST


def axis_operator(length):
    index = np.arange(length)
    signed = np.where(index < length // 2, index, index - length) * (2.0 * math.pi / length)
    phases = (index[:, None] * index[None, :] % length) * (2.0 * math.pi / length)
    first = (np.cos(phases) @ (0.5 * signed * signed)) / length
    return np.asarray(first[(index[:, None] - index[None, :]) % length], np.float32)


def far_first(count):
    return sorted(range(1, count), key=lambda k: -min(k, count - k))


def dot(left, right):
    return jnp.dot(left, right, precision=HIGH, preferred_element_type=jnp.float32)


def lanes(product):
    return jnp.sum(product, axis=0, keepdims=True)


def kernel(
    cy, cz, nx, fy, fz, poles,
    states_hbm, pot_hbm, dx_hbm, dy_hbm, dz_hbm,
    out_ref, corr_ref, energy_ref,
    own_b, far_b, v_ref, dx_ref, dy_ref, dz_ref, g_ref, s_ref, q_ref, u_ref, y_ref, dxs_ref, dxg_ref, far_u,
    ysend, yb, ymul, ymul2, yback, yback2, vsend, yv, z_order, g_order,
    zb, zq, zmul, zmul2, zback, zback2,
    acc, mine_sums, core_sums, chip_sums, parts, rows_ref,
    load_sem, send_sem, recv_sem,
):
    pole, my, mz = lax.axis_index("pole"), lax.axis_index("fy"), lax.axis_index("fz")
    partner = 1 - pole
    rows = cy * cz
    half = nx // 2
    col0, col1 = slice(0, half), slice(half, nx)

    def lane_block(index):
        return pl.ds(pl.multiple_of(index * half, half), half)

    def at_y(step):
        return (pole, lax.rem(my + step, fy), mz)

    def at_z(step):
        return (pole, my, lax.rem(mz + step, fz))

    def push(src, dst, place, slot):
        pltpu.make_async_remote_copy(
            src_ref=src,
            dst_ref=dst,
            send_sem=send_sem.at[slot],
            recv_sem=recv_sem.at[slot],
            device_id=place,
            device_id_type=MESH,
        ).start()

    def push_y(src, dst, step, slot):
        push(src.at[lax.rem(my + step, fy)], dst.at[my], at_y(step), slot)

    def push_z(src, dst, step, slot):
        push(src.at[lax.rem(mz + step, fz)], dst.at[mz], at_z(step), slot)

    def scatter_y(src, dst, slot):
        for step in far_first(fy):
            push_y(src, dst, step, slot)
        dst[my] = src[my]

    def scatter_z(src, dst, slot):
        for step in far_first(fz):
            push_z(src, dst, step, slot)
        dst[mz] = src[mz]

    def arrived(dst, count, slot):
        whole = dst.at[pl.ds(0, count)]
        pltpu.make_async_copy(whole, whole, recv_sem.at[slot]).wait()

    def sent(dst, count, slot):
        whole = dst.at[pl.ds(0, count)]
        pltpu.make_async_copy(whole, whole, send_sem.at[slot]).wait()

    parts[...] = jnp.zeros(parts.shape, jnp.float32)
    barrier = pltpu.get_barrier_semaphore()

    for step in far_first(fy):
        pl.semaphore_signal(barrier, inc=1, device_id=at_y(step), device_id_type=MESH)
    for step in far_first(fz):
        pl.semaphore_signal(barrier, inc=1, device_id=at_z(step), device_id_type=MESH)
    across = (partner, my, mz)
    pl.semaphore_signal(barrier, inc=1, device_id=across, device_id_type=MESH)

    def load(src, dst, slot):
        copy = pltpu.make_async_copy(src, dst, load_sem.at[slot])
        copy.start()
        return copy

    near = [load(states_hbm.at[c, :, :, lane_block(pole)], own_b.at[:, :, pl.ds(c * half, half)], c) for c in range(2)]
    rest = [
        load(states_hbm.at[c, :, :, lane_block(partner)], far_b.at[:, :, pl.ds(c * half, half)], 2 + c) for c in range(2)
    ]
    rest.append(load(pot_hbm.at[:, :, lane_block(pole)], v_ref.at[:, :, pl.ds(0, half)], 4))
    rest.append(load(pot_hbm.at[:, :, lane_block(partner)], v_ref.at[:, :, pl.ds(half, half)], 5))
    rest.append(load(dx_hbm, dx_ref, 6))
    rest.append(load(dz_hbm, dz_ref, 7))
    rest.append(load(dy_hbm, dy_ref, 8))
    for copy in near:
        copy.wait()
    for c in range(2):
        ysend[c] = jnp.swapaxes(own_b[:, :, c * half : (c + 1) * half], 0, 1)
    for copy in rest:
        copy.wait()

    def flat(ref):
        return ref[...].reshape(rows, nx)

    def column(ref, c):
        return ref[:, :, c * half : (c + 1) * half].reshape(-1, half)

    terms = [jnp.zeros((1, half), jnp.float32)] * 3

    def quadratic(left, right):
        terms[0] += lanes(left[0] * right[0])
        terms[1] += lanes(left[0] * right[1])
        terms[2] += lanes(left[1] * right[1])

    def symmetric(left, right):
        terms[0] += 2.0 * lanes(left[0] * right[0])
        terms[1] += lanes(left[0] * right[1] + left[1] * right[0])
        terms[2] += 2.0 * lanes(left[1] * right[1])

    v = v_ref[...].reshape(rows, nx)
    b = [column(own_b, c) for c in range(2)]
    g, s = [], []
    for c in range(2):
        whole = jnp.concatenate([b[c], column(far_b, c)], axis=1)
        g.append(dot(whole, dx_ref[...]))
        s.append(v * whole + g[c])
        here = slice(c * half, (c + 1) * half)
        s_ref[:, :, here] = s[c][:, col0].reshape(cy, cz, half)
        g_ref[:, :, here] = g[c][:, col0].reshape(cy, cz, half)
        q_ref[:, :, here] = (s[c][:, col0] + 0.5 * g[c][:, col0]).reshape(cy, cz, half)
    vsend[...] = jnp.swapaxes(v_ref[:, :, 0:half], 0, 1)
    g_order[...] = jnp.swapaxes(g_ref[...], 0, 1)

    pl.semaphore_wait(barrier, fy + fz - 1)
    scatter_y(ysend.at[0], yb.at[0], 0)
    scatter_y(ysend.at[1], yb.at[1], 11)
    scatter_z(own_b, zb, 1)
    scatter_y(vsend, yv, 2)
    scatter_z(q_ref, zq, 3)

    acc[0:1] = lanes(b[0] * b[0])
    acc[1:2] = lanes(b[0] * b[1])
    acc[2:3] = lanes(b[1] * b[1])
    acc[12:16] = jnp.zeros((4, 128), jnp.float32)
    for c in range(2):
        here = slice(c * half, (c + 1) * half)
        dxs_ref[:, :, here] = dot(s[c], dx_ref[:, col0]).reshape(cy, cz, half)
        dxg_ref[:, :, here] = dot(g[c], dx_ref[:, col0]).reshape(cy, cz, half)
    quadratic([s[c][:, col0] for c in range(2)], [column(dxs_ref, c) for c in range(2)])

    def y_column(c, slot, slot2):
        ymul[c] = dot(dy_ref[...], yb[c].reshape(-1, half)).reshape(fy, cy, half)
        ymul2[c] = dot(dy_ref[...], ymul[c].reshape(-1, half)).reshape(fy, cy, half)
        for step in far_first(fy):
            push_y(ymul.at[c], yback.at[c], step, slot)
            push_y(ymul2.at[c], yback2.at[c], step, slot2)
        yback[c, my] = ymul[c, my]
        yback2[c, my] = ymul2[c, my]

    arrived(yb.at[0], fy - 1, 0)
    y_column(0, 4, 6)
    arrived(yb.at[1], fy - 1, 11)
    y_column(1, 12, 13)
    arrived(zb, fz - 1, 1)
    zmul[...] = dot(dz_ref[...], flat(zb)).reshape(fz, cz, nx)
    scatter_z(zmul, zback, 5)
    z_twice = dot(dz_ref[...], flat(zmul))
    arrived(zq, fz - 1, 3)
    p = flat(zq) + flat(zmul)
    p_mul = dot(dz_ref[...], p)
    zmul2[...] = (4.0 * p_mul - z_twice).reshape(fz, cz, nx)
    scatter_z(zmul2, zback2, 7)
    quadratic([p[:, col0], p[:, col1]], [p_mul[:, col0], p_mul[:, col1]])
    arrived(yv, fy - 1, 2)
    h = [(yv[...] * yb[c]).reshape(-1, half) for c in range(2)]
    p_mul = [dot(dy_ref[...], h[c]) + ymul2[c].reshape(-1, half) for c in range(2)]
    quadratic([h[c] + ymul[c].reshape(-1, half) for c in range(2)], p_mul)

    arrived(zback, fz - 1, 5)
    for c, slot in ((0, 4), (1, 12)):
        arrived(yback.at[c], fy - 1, slot)
        y_ref[:, :, c * half : (c + 1) * half] = jnp.swapaxes(yback[c], 0, 1)
    u_ref[...] = s_ref[...] + zback[...] + y_ref[...]
    push(u_ref.at[:, :, lane_block(partner)], far_u, across, 10)
    u = [column(u_ref, c) for c in range(2)]
    acc[3:4] = lanes(b[0] * u[0])
    acc[4:5] = lanes(b[0] * u[1])
    acc[5:6] = lanes(b[1] * u[1])
    acc[6:7] = lanes(u[0] * u[0])
    acc[7:8] = lanes(u[0] * u[1])
    acc[8:9] = lanes(u[1] * u[1])
    quadratic(u, [v[:, col0] * u[c] for c in range(2)])
    y = [column(y_ref, c) for c in range(2)]
    symmetric([2.0 * column(dxs_ref, c) - 0.5 * column(dxg_ref, c) for c in range(2)], y)
    symmetric(
        [0.5 * column(dxs_ref, c) - 0.125 * column(dxg_ref, c) for c in range(2)],
        [column(zback, c) for c in range(2)],
    )
    z_order[...] = 1.5 * (g_order[...] + jnp.swapaxes(zback[...], 0, 1))
    arrived(zback2, fz - 1, 7)
    symmetric([0.5 * y[c] for c in range(2)], [column(zback2, c) for c in range(2)])
    left = [column(z_order, c) for c in range(2)]
    arrived(yback2.at[0], fy - 1, 6)
    right = yback2[0].reshape(-1, half)
    terms[0] += 2.0 * lanes(left[0] * right)
    terms[1] += lanes(left[1] * right)
    arrived(yback2.at[1], fy - 1, 13)
    right = yback2[1].reshape(-1, half)
    terms[1] += lanes(left[0] * right)
    terms[2] += 2.0 * lanes(left[1] * right)
    for i in range(3):
        acc[9 + i : 10 + i] = terms[i]

    lane = lax.broadcasted_iota(jnp.int32, (16, 128), 1)
    row = lax.broadcasted_iota(jnp.int32, (16, 128), 0)
    folded = acc[...]
    for shifts in ((32, 64, 96), (8, 16, 24)):
        folded = folded + sum(pltpu.roll(folded, shift, 1) for shift in shifts)
    mine_sums[...] = jnp.sum(jnp.where(lane // 8 == row, folded, 0.0), axis=0, keepdims=True)

    core = lax.rem(mz, 2)
    push(mine_sums, core_sums, (pole, my, mz + 1 - 2 * core), 8)
    size_x, size_y = 2 * poles, fz // 4
    place_x = [lax.rem(2 * pole + lax.rem(mz // 2, 2) + k, size_x) for k in range(size_x)]
    place_y = [lax.rem(mz // 4 + k, size_y) for k in range(size_y)]
    place_z = [lax.rem(my + k, fy) for k in range(fy)]
    pole_of = [x // 2 for x in place_x]
    low_of = [2 * lax.rem(x, 2) for x in place_x]
    chip = (my * size_y + mz // 4) * size_x + place_x[0]

    def hops(offset):
        return sum(min(k, n - k) for k, n in zip(offset, (size_x, size_y, fy)))

    offsets = sorted(
        ((x, y, z) for x in range(size_x) for y in range(size_y) for z in range(fy) if (x, y, z) != (0, 0, 0)),
        key=lambda offset: -hops(offset),
    )
    far_away = [offset for offset in offsets if hops(offset) >= hops(offsets[0]) - 3]

    def device(offset, which):
        x, y, z = offset
        return (pole_of[x], place_z[z], place_y[y] * 4 + low_of[x] + which)

    chips = size_x * size_y * fy
    mine_row = pl.ds(core * chips + chip, 1)
    pair_row = pl.ds(chip, 1)
    for offset in far_away:
        for which in range(2):
            push(mine_sums, parts.at[mine_row], device(offset, which), 9)

    whole_core = core_sums.at[pl.ds(0, 1)]
    pltpu.make_async_copy(whole_core, whole_core, recv_sem.at[8]).wait()
    chip_sums[...] = mine_sums[...] + core_sums[...]
    for offset in offsets[len(far_away) :]:
        push(chip_sums, parts.at[pair_row], device(offset, core), 9)
    parts[pair_row, :] = chip_sums[...]
    messages = len(offsets) + len(far_away)

    for slot, z_buffer in ((1, zb), (3, zq), (5, zback), (7, zback2)):
        sent(z_buffer, fz - 1, slot)
    for y_buffer, slots in ((yb, (0, 11)), (yback, (4, 12)), (yback2, (6, 13))):
        for c in range(2):
            sent(y_buffer.at[c], fy - 1, slots[c])
    sent(yv, fy - 1, 2)
    arrived(far_u, cy, 10)
    sent(far_u, cy, 10)
    pltpu.make_async_copy(whole_core, whole_core, send_sem.at[8]).wait()

    arrived(parts, messages, 9)
    total = jnp.sum(parts[0:chips] + parts[chips : 2 * chips], axis=0, keepdims=True)
    slim = lax.broadcasted_iota(jnp.int32, (8, 128), 1) < 8

    def totals(values):
        for i, value in enumerate(values):
            rows_ref[i : i + 1] = value
        summed = jnp.sum(jnp.where(slim, rows_ref[...], 0.0), axis=1, keepdims=True)
        rows_ref[...] = jnp.broadcast_to(summed, (8, 128))
        return [rows_ref[i : i + 1] for i in range(len(values))]

    l00, l01, l11, b00, b01, b11, u00, u01, u11, e00, e01, e11 = (
        pltpu.roll(total, (128 - 8 * i) % 128, 1) if i else total for i in range(12)
    )
    m00, m01, m11, h00, h11 = totals([l00, l01, l11, b00, b11])
    mu = [h00 / m00, h11 / m11]
    w00, w01, w11, e00, e01, e11, c01, c10 = totals(
        [
            u00 - mu[0] * (2.0 * b00 - mu[0] * l00),
            u01 - (mu[0] + mu[1]) * b01 + mu[0] * mu[1] * l01,
            u11 - mu[1] * (2.0 * b11 - mu[1] * l11),
            e00 - mu[0] * (2.0 * u00 - mu[0] * b00),
            e01 - (mu[0] + mu[1]) * u01 + mu[0] * mu[1] * b01,
            e11 - mu[1] * (2.0 * u11 - mu[1] * b11),
            b01 - mu[1] * l01,
            b01 - mu[0] * l01,
        ]
    )

    top = 1.5 * math.pi**2 + 3.0

    def factors(mean, norm, ww, whw):
        nu = jnp.where(ww > 0.0, jnp.clip(whw / jnp.where(ww > 0.0, ww, 1.0), 0.0, top), mean)
        t2 = jnp.maximum(ww, 0.0) / norm
        p, q = mean - 1.0, nu - 1.0
        trace, det = p + q, p * q - t2
        real, imag = det * det - 1.0, 2.0 * det - trace * trace
        size = real * real + imag * imag
        return ((det - q * trace) * imag - real) / size, trace * imag / size

    per_cell = 1.0 / float(nx * cy * fy * cz * fz)

    def gram(ref, upper, cross, lower):
        lane = lax.broadcasted_iota(jnp.int32, (1, 128), 1)
        ref[0:1, :] = (jnp.where(lane == 0, upper, cross) * per_cell)[:, 0:2]
        ref[1:2, :] = (jnp.where(lane == 0, cross, lower) * per_cell)[:, 0:2]

    a0, f0 = factors(mu[0], m00, w00, e00)
    a1, f1 = factors(mu[1], m11, w11, e11)
    first = pole == 0
    a, f = jnp.where(first, a0, a1), jnp.where(first, f0, f1)
    my_mu = jnp.where(first, mu[0], mu[1])
    column_block = lane_block(pole)
    for block, base, applied in (
        (lane_block(pole), own_b[:, :, column_block], u_ref[:, :, column_block]),
        (lane_block(partner), far_b[:, :, column_block], far_u[...]),
    ):
        out_ref[0, :, :, block] = a * base + f * (applied - my_mu * base)
    cross = a0 * a1 * m01 + a0 * f1 * c01 + f0 * a1 * c10 + f0 * f1 * w01
    gram(corr_ref, a0 * a0 * m00 + f0 * f0 * w00, cross, a1 * a1 * m11 + f1 * f1 * w11)
    cross = (
        a0 * a1 * (c01 + mu[1] * m01)
        + a0 * f1 * (w01 + mu[0] * c01)
        + f0 * a1 * (w01 + mu[1] * c10)
        + f0 * f1 * e01
    )
    gram(
        energy_ref,
        a0 * a0 * mu[0] * m00 + 2.0 * a0 * f0 * w00 + f0 * f0 * e00,
        cross,
        a1 * a1 * mu[1] * m11 + 2.0 * a1 * f1 * w11 + f1 * f1 * e11,
    )
    sent(parts, messages, 9)


def local(states, potential):
    columns, cy, cz, nx = states.shape
    fy, fz, poles = lax.axis_size("fy"), lax.axis_size("fz"), lax.axis_size("pole")
    half = nx // 2
    f32 = jnp.float32
    in_vmem = pl.BlockSpec(memory_space=pltpu.VMEM)
    in_hbm = pl.BlockSpec(memory_space=pl.ANY)

    def vmem(*shape):
        return pltpu.VMEM(shape, f32)

    x_block, y_block, z_block = vmem(cy, cz, nx), vmem(fy, cy, nx), vmem(fz, cz, nx)
    filtered, corr, energy = pl.pallas_call(
        functools.partial(kernel, cy, cz, nx, fy, fz, poles),
        out_shape=(
            jax.ShapeDtypeStruct((1, cy, cz, nx), f32),
            jax.ShapeDtypeStruct((columns, columns), f32),
            jax.ShapeDtypeStruct((columns, columns), f32),
        ),
        in_specs=[in_hbm] * 5,
        out_specs=(in_vmem,) * 3,
        scratch_shapes=[
            *[x_block] * 3,
            vmem(nx, nx), vmem(cy * fy, cy * fy), vmem(cz * fz, cz * fz),
            *[x_block] * 7, vmem(cy, cz, half),
            *[vmem(columns, fy, cy, half)] * 6, vmem(fy, cy, half), vmem(fy, cy, half), y_block, y_block,
            *[z_block] * 6,
            vmem(16, 128), vmem(1, 128), vmem(1, 128), vmem(1, 128), vmem(fy * poles * fz, 128), vmem(8, 128),
            pltpu.SemaphoreType.DMA((9,)),
            pltpu.SemaphoreType.DMA((14,)),
            pltpu.SemaphoreType.DMA((14,)),
        ],
        compiler_params=pltpu.CompilerParams(
            collective_id=0, has_side_effects=True, vmem_limit_bytes=32 * 1024 * 1024
        ),
    )(
        *(
            pltpu.with_memory_space_constraint(operand, pltpu.HBM)
            for operand in (
                states,
                potential,
                jnp.asarray(axis_operator(nx)),
                jnp.asarray(axis_operator(cy * fy)),
                jnp.asarray(axis_operator(cz * fz)),
            )
        )
    )
    outs = (filtered, corr, energy)
    return pl.pallas_call(
        store,
        out_shape=tuple(jax.ShapeDtypeStruct(out.shape, f32) for out in outs),
        in_specs=[in_vmem] * 3,
        out_specs=(in_hbm,) * 3,
        scratch_shapes=[pltpu.SemaphoreType.DMA((3,))],
    )(*(pltpu.with_memory_space_constraint(out, pltpu.VMEM) for out in outs))


def store(filtered, corr, energy, filtered_out, corr_out, energy_out, sem):
    pairs = ((filtered, filtered_out), (corr, corr_out), (energy, energy_out))
    copies = [pltpu.make_async_copy(src, dst, sem.at[i]) for i, (src, dst) in enumerate(pairs)]
    for copy in copies:
        copy.start()
    for copy in copies:
        copy.wait()


def solution(mesh):
    placed = (P(None, "fy", "fz", None), P("fy", "fz", None))
    return jax.shard_map(
        local,
        mesh=mesh,
        in_specs=placed,
        out_specs=(P("pole", "fy", "fz", None), P(), P()),
        check_vma=False,
    )
```
